256 devices in a mesh: section: 8 (over z_lo, x), seq: 32 (over y, z_hi, core).
Axes of the slice: x: 4, y: 4, z: 8 (z_hi: 4, z_lo: 2; z = z_hi * 2 + z_lo), core: 2. Of those that a mesh axis runs over, the one named last changes fastest.
Arguments:
- latents: bfloat16 [4, 2048, 1024], P(None, 'seq'), may hold values from -6 to 6
- norm_gain: float32 [8, 1024], P('section'), may hold values from 0.1 to 1.9
- qkv_weight: bfloat16 [8, 1024, 3072], P('section', 'seq'), may hold values from -1 to 1
- proj_weight: bfloat16 [8, 1024, 1024], P('section', 'seq'), may hold values from -0.1875 to 0.1875
- merge_weight: bfloat16 [8, 1024, 1024], P('section', 'seq'), may hold values from -0.125 to 0.125
Outputs:
- denoised: bfloat16 [4, 2048, 1024], P(None, 'seq', 'section')
The draws below stay inside these ranges and needn't reach their ends.
All inputs are finite; a program needn't handle non-finite values.
Results may differ from the reference program's by a relative error of at most 0.017.
Values may be sent and summed in bfloat16 or wider, within the bound.
A program may use at most 64 MiB of HBM per device.

```python
import jax
import jax.numpy as jnp
from jax import lax

D = 1024
HEADS = 16
HEAD_DIM = 64
WINDOWS = 4
WINDOW = 2048
N_SECTION = 8


def draw_qkv_weight(key, part):
    drawn = jax.random.normal(key, (N_SECTION, D, 3 * D), jnp.float32) * D ** (-0.5)
    return jnp.clip(drawn, -1.0, 1.0).astype(jnp.bfloat16)


def block_levels(key, dims, shards, least, high):
    loudness = 1.0
    for position, shards_of in shards:
        heights = jax.random.uniform(jax.random.fold_in(jax.random.fold_in(key, 6), position), (shards_of,), jnp.float32, least / len(shards), high / len(shards))
        loudness = loudness * jnp.repeat(jnp.exp(heights), dims[position] // shards_of).reshape((-1,) + (1,) * (len(dims) - 1 - position))
    return loudness


def scatter_about(own_key, shape, scale, bound, cuts=(), held_as=jnp.bfloat16):
    values = scale * jax.random.normal(own_key, shape, jnp.float32)
    if cuts:
        values = values * block_levels(own_key, shape, cuts, -0.22, 0.18)
    return jnp.clip(values, -bound, bound).astype(held_as)


def setup_inputs(seed: int = 0) -> dict:
    key_list = jax.random.split(jax.random.key(seed), 6)
    latents = scatter_about(key_list[0], (WINDOWS, WINDOW, D), 1.0, 6.0, ((1, 32),))
    norm_gain = jnp.clip(1.0 + 0.18 * jax.random.normal(key_list[1], (N_SECTION, D), jnp.float32), 0.1, 1.9)
    qkv_weight = draw_qkv_weight(jax.random.fold_in(key_list[5], 71), 0)
    proj_weight = scatter_about(key_list[3], (N_SECTION, D, D), D ** -0.5, 0.1875, ((0, 8), (1, 32)))
    merge_weight = scatter_about(key_list[4], (N_SECTION, D, D), (2 * D) ** -0.5, 0.125, ((0, 8), (1, 32)))
    return dict(latents=latents, norm_gain=norm_gain, qkv_weight=qkv_weight, proj_weight=proj_weight, merge_weight=merge_weight)


EPSILON = 1e-05

def layer_norm(hidden, gain_row):
    values = hidden.astype(jnp.float32)
    center = values - lax.optimization_barrier(jnp.mean(values, axis=-1, keepdims=True))
    spread = lax.optimization_barrier(jnp.mean(center * center, axis=-1, keepdims=True))
    return (center * lax.rsqrt(spread + EPSILON) * gain_row).astype(jnp.bfloat16)

def attend_head(operands):
    query_head, key_head, value_head = operands
    scores = jnp.dot(query_head, key_head.T, preferred_element_type=jnp.float32) * HEAD_DIM ** (-0.5)
    row_max = lax.optimization_barrier(jnp.max(scores, axis=-1, keepdims=True))
    weights = jnp.exp(scores - row_max)
    totals = lax.optimization_barrier(jnp.sum(weights, axis=-1, keepdims=True))
    probs = weights.astype(jnp.bfloat16)
    mixed = jnp.dot(probs, value_head, preferred_element_type=jnp.float32)
    return (mixed / totals).astype(jnp.bfloat16)

def block(hidden, gain_row, w_qkv, w_proj):
    normed = layer_norm(hidden, gain_row)
    packed = jnp.dot(normed, w_qkv, preferred_element_type=jnp.float32).astype(jnp.bfloat16)
    rows = hidden.shape[0]

    def split_heads(columns):
        return columns.reshape(rows, HEADS, HEAD_DIM).transpose(1, 0, 2)
    queries = split_heads(packed[:, :D])
    keys_all = split_heads(packed[:, D:2 * D])
    values_all = split_heads(packed[:, 2 * D:])
    mixed = lax.map(attend_head, (queries, keys_all, values_all))
    mixed = mixed.transpose(1, 0, 2).reshape(rows, D)
    update = jnp.dot(mixed, w_proj, preferred_element_type=jnp.float32)
    return (hidden.astype(jnp.float32) + update).astype(jnp.bfloat16)

def one_window(hidden, norm_gain, qkv_weight, proj_weight, merge_weight):
    skip_terms = []
    midpoint = N_SECTION // 2
    for section_no in range(N_SECTION):
        if section_no >= midpoint:
            joined = jnp.dot(hidden, merge_weight[section_no], preferred_element_type=jnp.float32)
            hidden = (joined + skip_terms[N_SECTION - 1 - section_no].astype(jnp.float32)).astype(jnp.bfloat16)
        hidden = block(hidden, norm_gain[section_no], qkv_weight[section_no], proj_weight[section_no])
        if section_no < midpoint:
            skip_terms.append(jnp.dot(hidden, merge_weight[section_no], preferred_element_type=jnp.float32).astype(jnp.bfloat16))
    return hidden

def reference(latents, norm_gain, qkv_weight, proj_weight, merge_weight):
    outputs = [one_window(latents[window_no], norm_gain, qkv_weight, proj_weight, merge_weight) for window_no in range(WINDOWS)]
    return jnp.stack(outputs, axis=0)
```

```python
import functools
import math

import jax
import jax.numpy as jnp
from jax import lax
from jax.experimental import pallas as pl
from jax.experimental.pallas import tpu as pltpu
from jax.sharding import PartitionSpec as P

HEAD_DIM = 64
SLICE = 128
CORES = 2
EPSILON = 1e-05
F32 = jnp.float32
BF16 = jnp.bfloat16


def rcopy(src, dst, send, recv, section, seq):
    return pltpu.make_async_remote_copy(
        src_ref=src,
        dst_ref=dst,
        send_sem=send,
        recv_sem=recv,
        device_id={"section": section, "seq": seq},
        device_id_type=pl.DeviceIdType.MESH,
    )


def kernel(ns, ny, nz, tok, lat_ref, w_ref, out_ref, H, U, A, KV, S, W, skips, O,
           p1s, p1r, zs, zr, ys, yr, cs, cr, hs, hr, us, ur, as_, ar, kvs, kvr, os_, or_):
    nc = CORES
    rows = nz * tok
    nt = ny * nc
    dim = ns * SLICE
    sec = lax.axis_index("section")
    seq = lax.axis_index("seq")
    y = seq // (nz * nc)
    z = (seq // nc) % nz
    c = seq % nc
    t = y * nc + c

    def seq_of(y_, z_, c_):
        return y_ * (nz * nc) + z_ * nc + c_

    def sec_peer(d):
        return lax.rem(sec + d, ns)

    def z_peer(d):
        return lax.rem(z + d, nz)

    def y_peer(d):
        return lax.rem(y + d, ny)

    t_offsets = [(dy, dc) for dy in range(ny) for dc in range(nc)]
    t_offsets.sort(key=lambda o: (min(o[0], ny - o[0]), o[1]))

    def t_peer(o):
        return lax.rem(y + o[0], ny), lax.rem(c + o[1], nc)

    barrier = pltpu.get_barrier_semaphore()
    count = 0
    for d in range(1, ns):
        pl.semaphore_signal(barrier, inc=1, device_id={"section": sec_peer(d), "seq": seq}, device_id_type=pl.DeviceIdType.MESH)
        count += 1
    for d in range(1, nz):
        pl.semaphore_signal(barrier, inc=1, device_id={"section": sec, "seq": seq_of(y, z_peer(d), c)}, device_id_type=pl.DeviceIdType.MESH)
        count += 1
    for o in t_offsets[1:]:
        y_, c_ = t_peer(o)
        pl.semaphore_signal(barrier, inc=1, device_id={"section": sec, "seq": seq_of(y_, z, c_)}, device_id_type=pl.DeviceIdType.MESH)
        count += 1
    pl.semaphore_wait(barrier, count)

    def first_copies():
        return [rcopy(w_ref.at[sec_peer(d)], W.at[sec, y, z, c], p1s.at[d - 1], p1r.at[sec], sec_peer(d), seq) for d in range(1, ns)]

    def first_wait(s):
        @pl.when(s != sec)
        def _():
            rcopy(w_ref.at[s], W.at[s, y, z, c], p1s.at[0], p1r.at[s], sec, seq).wait_recv()

    def z_copies(s):
        return [rcopy(W.at[s, y, z, c], W.at[s, y, z, c], zs.at[d - 1], zr.at[s, z], sec, seq_of(y, z_peer(d), c)) for d in range(1, nz)]

    def z_wait(s):
        for d in range(1, nz):
            p = z_peer(d)
            rcopy(W.at[s, y, p, c], W.at[s, y, p, c], zs.at[d - 1], zr.at[s, p], sec, seq).wait_recv()

    def y_copies(s):
        return [rcopy(W.at[s, y, :, c], W.at[s, y, :, c], ys.at[d - 1], yr.at[s, y], sec, seq_of(y_peer(d), z, c)) for d in range(1, ny)]

    def y_wait(s):
        for d in range(1, ny):
            p = y_peer(d)
            rcopy(W.at[s, p, :, c], W.at[s, p, :, c], ys.at[d - 1], yr.at[s, p], sec, seq).wait_recv()

    def c_copy(s):
        return rcopy(W.at[s, :, :, c], W.at[s, :, :, c], cs.at[0], cr.at[s], sec, seq_of(y, z, 1 - c))

    def c_wait(s):
        rcopy(W.at[s, :, :, 1 - c], W.at[s, :, :, 1 - c], cs.at[0], cr.at[s], sec, seq).wait_recv()

    def gather_copies(buf, ssem, rsem):
        return [rcopy(buf.at[sec], buf.at[sec], ssem.at[d - 1], rsem.at[sec], sec_peer(d), seq) for d in range(1, ns)]

    def gather_wait(buf, ssem, rsem):
        for d in range(1, ns):
            p = sec_peer(d)
            rcopy(buf.at[p], buf.at[p], ssem.at[d - 1], rsem.at[p], sec, seq).wait_recv()

    def kv_copies(par):
        out = []
        for i, o in enumerate(t_offsets[1:]):
            y_, c_ = t_peer(o)
            out.append(rcopy(KV.at[par, t], KV.at[par, t], kvs.at[i], kvr.at[par, t], sec, seq_of(y_, z, c_)))
        return out

    def start(copies):
        for copy in copies:
            copy.start()

    def wait_send(copies):
        for copy in copies:
            copy.wait_send()

    start(first_copies())
    W[sec, y, z, c] = w_ref[sec]
    lat_copies = [
        rcopy(lat_ref.at[z_peer(d)], H.at[sec, pl.ds(z * tok, tok)], os_.at[d - 1], or_.at[z], sec, seq_of(y, z_peer(d), c))
        for d in range(1, nz)
    ]
    start(lat_copies)
    H[sec, pl.ds(pl.multiple_of(z * tok, tok), tok), :] = lat_ref[z]
    first_wait(0)
    start(z_copies(0))
    for d in range(1, nz):
        p = z_peer(d)
        rcopy(lat_ref.at[p], H.at[sec, pl.ds(p * tok, tok)], os_.at[d - 1], or_.at[p], sec, seq).wait_recv()
    z_wait(0)
    start(y_copies(0))
    wait_send(z_copies(0))
    wait_send(lat_copies)
    for s in range(1, ns):
        first_wait(s)
    wait_send(first_copies())
    y_wait(0)
    wait_send(y_copies(0))
    c_copy(0).start()

    def weights(s, lo, hi):
        return W[s, :, :, :, :, lo:hi].reshape(dim, hi - lo)

    def whole(buf):
        return jnp.concatenate([buf[p] for p in range(ns)], axis=1)

    lane = lax.broadcasted_iota(jnp.int32, (rows, SLICE), 1)

    def block(s, decoder):
        par = lax.rem(s, 2)
        more = s + 1 < ns
        start(gather_copies(H, hs, hr))

        @pl.when(more)
        def _():
            start(z_copies(s + 1))

        c_wait(s)
        c_copy(s).wait_send()
        gather_wait(H, hs, hr)
        if decoder:
            @pl.when(s == ns // 2)
            def _():
                skips[s - 1] = jnp.dot(whole(H), weights(s - 1, 512, 640), preferred_element_type=F32).astype(BF16)

            merged = jnp.dot(whole(H), weights(s, 512, 640), preferred_element_type=F32)
            U[sec] = (merged + skips[ns - 1 - s].astype(F32)).astype(BF16)
            start(gather_copies(U, us, ur))
            gather_wait(U, us, ur)
            src = U
        else:
            src = H
        total = jnp.zeros((rows, SLICE), F32)
        for p in range(ns):
            total = total + src[p].astype(F32)
        mean = jnp.sum(total, axis=-1, keepdims=True) * (1.0 / dim)
        total = jnp.zeros((rows, SLICE), F32)
        for p in range(ns):
            center = src[p].astype(F32) - mean
            total = total + center * center
        spread = jnp.sum(total, axis=-1, keepdims=True) * (1.0 / dim)
        inverse = lax.rsqrt(spread + EPSILON)
        normed = jnp.concatenate([((src[p].astype(F32) - mean) * inverse).astype(BF16) for p in range(ns)], axis=1)
        kv = jnp.dot(normed, weights(s, 128, 384), preferred_element_type=F32)
        KV[par, t] = kv.astype(BF16)
        start(kv_copies(par))
        q = jnp.dot(normed, weights(s, 0, 128), preferred_element_type=F32)
        q_heads = [jnp.where(lane < HEAD_DIM, q, 0.0).astype(BF16), jnp.where(lane < HEAD_DIM, 0.0, q).astype(BF16)]

        @pl.when(more)
        def _():
            z_wait(s + 1)
            start(y_copies(s + 1))
            wait_send(z_copies(s + 1))

        if not decoder:
            @pl.when(s >= 1)
            def _():
                skips[s - 1] = jnp.dot(whole(H), weights(s - 1, 512, 640), preferred_element_type=F32).astype(BF16)

        wait_send(gather_copies(H, hs, hr))
        if decoder:
            wait_send(gather_copies(U, us, ur))

        tops = [None, None]
        for i, o in enumerate(t_offsets):
            y_, c_ = t_peer(o)
            slot = y_ * nc + c_
            if i > 0:
                rcopy(KV.at[par, slot], KV.at[par, slot], kvs.at[i - 1], kvr.at[par, slot], sec, seq).wait_recv()
            keys = KV[par, slot, :, 0:SLICE]
            for h in range(2):
                scores = lax.dot_general(q_heads[h], keys, (((1,), (1,)), ((), ())), preferred_element_type=F32)
                S[h, i] = scores
                top = jnp.max(scores, axis=-1, keepdims=True)
                tops[h] = top if tops[h] is None else jnp.maximum(tops[h], top)
        mixes = []
        for h in range(2):
            acc = jnp.zeros((rows, SLICE), F32)
            sums = jnp.zeros((rows, 1), F32)
            for i, o in enumerate(t_offsets):
                y_, c_ = t_peer(o)
                slot = y_ * nc + c_
                e = jnp.exp2(S[h, i] - tops[h])
                sums = sums + jnp.sum(e, axis=-1, keepdims=True)
                acc = acc + jnp.dot(e.astype(BF16), KV[par, slot, :, SLICE:2 * SLICE], preferred_element_type=F32)
            mixes.append(acc / sums)
        A[sec] = jnp.where(lane < HEAD_DIM, mixes[0], mixes[1]).astype(BF16)
        start(gather_copies(A, as_, ar))
        wait_send(kv_copies(par))

        @pl.when(more)
        def _():
            y_wait(s + 1)
            wait_send(y_copies(s + 1))
            c_copy(s + 1).start()

        gather_wait(A, as_, ar)
        update = jnp.dot(whole(A), weights(s, 384, 512), preferred_element_type=F32)
        H[sec] = (src[sec].astype(F32) + update).astype(BF16)
        wait_send(gather_copies(A, as_, ar))

    def encoder_step(s, carry):
        block(s, False)
        return carry

    def decoder_step(s, carry):
        block(s, True)
        return carry

    lax.fori_loop(0, ns // 2, encoder_step, 0)
    lax.fori_loop(ns // 2, ns, decoder_step, 0)

    out_copies = [
        rcopy(H.at[sec, pl.ds(z_peer(d) * tok, tok)], O.at[z], os_.at[d - 1], or_.at[z], sec, seq_of(y, z_peer(d), c))
        for d in range(1, nz)
    ]
    start(out_copies)
    O[z] = H[sec, pl.ds(pl.multiple_of(z * tok, tok), tok), :]
    for d in range(1, nz):
        p = z_peer(d)
        rcopy(O.at[p], O.at[p], os_.at[d - 1], or_.at[p], sec, seq).wait_recv()
    out_ref[...] = O[...]
    wait_send(out_copies)


def body(latents, norm_gain, qkv_weight, proj_weight, merge_weight):
    windows, tok, dim = latents.shape
    ns = lax.axis_size("section")
    nseq = lax.axis_size("seq")
    nz = windows
    ny = nseq // (nz * CORES)
    part = dim // nseq
    sec = lax.axis_index("section")
    seq = lax.axis_index("seq")
    rows = nz * tok
    nt = ny * CORES
    lat = lax.dynamic_slice_in_dim(latents, sec * SLICE, SLICE, axis=2)
    gain = lax.dynamic_slice_in_dim(norm_gain[0], seq * part, part)[:, None]
    scale = jnp.where(jnp.arange(3 * dim) < dim, HEAD_DIM ** (-0.5) * math.log2(math.e), 1.0).astype(F32)
    folded = (qkv_weight[0].astype(F32) * gain * scale[None, :]).astype(BF16)
    packed = jnp.concatenate([folded, proj_weight[0], merge_weight[0]], axis=1)
    packed = packed.reshape(part, 5, ns, SLICE).transpose(2, 0, 1, 3).reshape(ns, part, 5 * SLICE)
    dma = pltpu.SemaphoreType.DMA
    vmem = pl.BlockSpec(memory_space=pltpu.VMEM)
    return pl.pallas_call(
        functools.partial(kernel, ns, ny, nz, tok),
        out_shape=jax.ShapeDtypeStruct((nz, tok, SLICE), BF16),
        in_specs=[vmem, vmem],
        out_specs=vmem,
        scratch_shapes=[
            pltpu.VMEM((ns, rows, SLICE), BF16),
            pltpu.VMEM((ns, rows, SLICE), BF16),
            pltpu.VMEM((ns, rows, SLICE), BF16),
            pltpu.VMEM((2, nt, rows, 2 * SLICE), BF16),
            pltpu.VMEM((2, nt, rows, rows), F32),
            pltpu.VMEM((ns, ny, nz, CORES, part, 5 * SLICE), BF16),
            pltpu.VMEM((ns // 2, rows, SLICE), BF16),
            pltpu.VMEM((nz, tok, SLICE), BF16),
            dma((ns - 1,)), dma((ns,)),
            dma((nz - 1,)), dma((ns, nz)),
            dma((ny - 1,)), dma((ns, ny)),
            dma((1,)), dma((ns,)),
            dma((ns - 1,)), dma((ns,)),
            dma((ns - 1,)), dma((ns,)),
            dma((ns - 1,)), dma((ns,)),
            dma((nt - 1,)), dma((2, nt)),
            dma((nz - 1,)), dma((nz,)),
        ],
        compiler_params=pltpu.CompilerParams(collective_id=0, has_side_effects=True, vmem_limit_bytes=48 * 1024 * 1024),
        name="blocks",
    )(lat, packed)


def solution(mesh):
    placed = (
        P(None, "seq", None),
        P("section", None),
        P("section", "seq", None),
        P("section", "seq", None),
        P("section", "seq", None),
    )
    return jax.shard_map(
        body, mesh=mesh, in_specs=placed, out_specs=P(None, "seq", "section"), check_vma=False
    )
```

```python
import functools
import math

import jax
import jax.numpy as jnp
from jax import lax
from jax.experimental import pallas as pl
from jax.experimental.pallas import tpu as pltpu
from jax.sharding import PartitionSpec as P

HEAD_DIM = 64
SLICE = 128
CORES = 2
EPSILON = 1e-05
F32 = jnp.float32
BF16 = jnp.bfloat16
MESH = pl.DeviceIdType.MESH


def rcopy(src, dst, send, recv, section, seq):
    return pltpu.make_async_remote_copy(
        src_ref=src,
        dst_ref=dst,
        send_sem=send,
        recv_sem=recv,
        device_id={"section": section, "seq": seq},
        device_id_type=MESH,
    )


def start(copies):
    for copy in copies:
        copy.start()


def wait_send(copies):
    for copy in copies:
        copy.wait_send()


def wait_recv(copies):
    for copy in copies:
        copy.wait_recv()


def kernel(ns, ny, nz, tok, lat_ref, w_ref, m_ref, p_ref, out_ref,
           H, A, KV, S, R, W, MD, WP, skips, O,
           p1s, p1r, m1s, m1r, q1s, q1r, wzs, wzr, wys, wyr, wcs, wcr,
           mzs, mzr, mys, myr, mcs, mcr, hs, hr, as_, ar, kvs, kvr, rls, os_, or_):
    nc = CORES
    nt = ny * nc
    mid = ns // 2
    dim = ns * SLICE
    zh = nz // 2
    half = zh * tok
    sec = lax.axis_index("section")
    seq = lax.axis_index("seq")
    y = seq // (nz * nc)
    z = (seq // nc) % nz
    c = seq % nc
    t = y * nc + c

    def seq_of(y_, z_, c_):
        return y_ * (nz * nc) + z_ * nc + c_

    def sec_peer(d):
        return lax.rem(sec + d, ns)

    def z_peer(d):
        return lax.rem(z + d, nz)

    def y_peer(d):
        return lax.rem(y + d, ny)

    y_order = sorted(range(1, ny), key=lambda d: min(d, ny - d))
    sibling = seq_of(y, z, 1 - c)

    barrier = pltpu.get_barrier_semaphore()
    greeted = [(sec_peer(d), seq) for d in range(1, ns)]
    greeted += [(sec, seq_of(y, z_peer(d), c)) for d in range(1, nz)]
    greeted += [(sec, seq_of(y_peer(d), z, c)) for d in range(1, ny)]
    greeted += [(sec, sibling)]
    for section_, seq_ in greeted:
        pl.semaphore_signal(barrier, inc=1, device_id={"section": section_, "seq": seq_}, device_id_type=MESH)
    pl.semaphore_wait(barrier, len(greeted))

    def first_copies():
        out = []
        for d in range(1, ns):
            p = sec_peer(d)
            out.append(rcopy(w_ref.at[p], W.at[sec, y, z, c], p1s.at[d - 1], p1r.at[sec], p, seq))
            out.append(rcopy(m_ref.at[p], MD.at[sec % mid, y, z, c, sec // mid], m1s.at[d - 1], m1r.at[sec], p, seq))
        return out

    def first_wait(s):
        @pl.when(sec != s)
        def _():
            rcopy(w_ref.at[s], W.at[s, y, z, c], p1s.at[0], p1r.at[s], sec, seq).wait_recv()

    def merge_wait(s):
        @pl.when(sec != s)
        def _():
            rcopy(m_ref.at[s], MD.at[s % mid, y, z, c, s // mid], m1s.at[0], m1r.at[s], sec, seq).wait_recv()

    composed = (sec >= mid - 1) & (sec < ns - 1)

    def proj_copies():
        return [rcopy(p_ref, WP.at[sec - (mid - 1)], q1s.at[d - 1], q1r.at[sec - (mid - 1)], sec_peer(d), seq) for d in range(1, ns)]

    def proj_wait(i):
        @pl.when(sec != i + mid - 1)
        def _():
            rcopy(p_ref, WP.at[i], q1s.at[0], q1r.at[i], sec, seq).wait_recv()

    w_sems = (wzs, wzr, wys, wyr, wcs, wcr)
    m_sems = (mzs, mzr, mys, myr, mcs, mcr)

    def z_copies(ref, sems, s):
        return [rcopy(ref.at[s, y, z, c], ref.at[s, y, z, c], sems[0].at[d - 1], sems[1].at[s, z], sec, seq_of(y, z_peer(d), c)) for d in range(1, nz)]

    def z_waits(ref, sems, s):
        wait_recv([rcopy(ref.at[s, y, z_peer(d), c], ref.at[s, y, z_peer(d), c], sems[0].at[d - 1], sems[1].at[s, z_peer(d)], sec, seq) for d in range(1, nz)])

    def y_copies(ref, sems, s):
        return [rcopy(ref.at[s, y, :, c], ref.at[s, y, :, c], sems[2].at[d - 1], sems[3].at[s, y], sec, seq_of(y_peer(d), z, c)) for d in y_order]

    def y_waits(ref, sems, s):
        wait_recv([rcopy(ref.at[s, y_peer(d), :, c], ref.at[s, y_peer(d), :, c], sems[2].at[d - 1], sems[3].at[s, y_peer(d)], sec, seq) for d in y_order])

    def c_copy(ref, sems, s):
        return rcopy(ref.at[s, :, :, c], ref.at[s, :, :, c], sems[4].at[0], sems[5].at[s], sec, sibling)

    def c_wait(ref, sems, s):
        c_copy(ref, sems, s).wait_send()
        rcopy(ref.at[s, :, :, 1 - c], ref.at[s, :, :, 1 - c], sems[4].at[0], sems[5].at[s], sec, seq).wait_recv()

    def stage_z(ref, sems, s):
        start(z_copies(ref, sems, s))

    def stage_y(ref, sems, s):
        z_waits(ref, sems, s)
        start(y_copies(ref, sems, s))
        wait_send(z_copies(ref, sems, s))

    def stage_c(ref, sems, s):
        y_waits(ref, sems, s)
        c_copy(ref, sems, s).start()
        wait_send(y_copies(ref, sems, s))

    def prefetch(stage, s):
        @pl.when(s < ns - 1)
        def _():
            stage(W, w_sems, s + 1)

        @pl.when(s < mid)
        def _():
            stage(MD, m_sems, s)

    def gather_copies(buf, ssem, rsem, g):
        return [rcopy(buf.at[g, sec], buf.at[g, sec], ssem.at[g, d - 1], rsem.at[g, sec], sec_peer(d), seq) for d in range(1, ns)]

    def gather_wait(buf, ssem, rsem, g):
        wait_recv([rcopy(buf.at[g, sec_peer(d)], buf.at[g, sec_peer(d)], ssem.at[g, d - 1], rsem.at[g, sec_peer(d)], sec, seq) for d in range(1, ns)])

    def kv_copies(par, g):
        out = [rcopy(KV.at[par, g, t], KV.at[par, g, t], kvs.at[g, d], kvr.at[par, g, t], sec, seq_of(y_peer(d), z, c)) for d in y_order]
        out.append(rcopy(KV.at[par, g, t], KV.at[par, g, t], kvs.at[g, 0], kvr.at[par, g, t], sec, sibling))
        return out

    def kv_slot(d, dc):
        return y_peer(d) * nc + (c if dc == 0 else 1 - c)

    def kv_wait(par, g, d, dc):
        slot = kv_slot(d, dc)
        rcopy(KV.at[par, g, slot], KV.at[par, g, slot], kvs.at[g, 0], kvr.at[par, g, slot], sec, seq).wait_recv()

    def relay(par, g, d):
        slot = kv_slot(d, 0)
        return rcopy(KV.at[par, g, slot], KV.at[par, g, slot], rls.at[g, d], kvr.at[par, g, slot], sec, sibling)

    def rows_of(z_):
        return pl.ds(lax.rem(z_, zh) * tok, tok)

    def local_rows(z_):
        return pl.ds(pl.multiple_of(lax.rem(z_, zh) * tok, tok), tok)

    start(first_copies())
    lat_copies = [
        rcopy(lat_ref.at[z_peer(d)], H.at[z // zh, sec, rows_of(z)], os_.at[d - 1], or_.at[z], sec, seq_of(y, z_peer(d), c))
        for d in range(1, nz)
    ]
    start(lat_copies)
    W[sec, y, z, c] = w_ref[sec]
    MD[sec % mid, y, z, c, sec // mid] = m_ref[sec]
    H[z // zh, sec, local_rows(z), :] = lat_ref[z]

    @pl.when(composed)
    def _():
        start(proj_copies())
        WP[sec - (mid - 1)] = p_ref[...]

    first_wait(0)
    stage_z(W, w_sems, 0)
    for d in range(1, nz):
        p = z_peer(d)
        rcopy(lat_ref.at[p], H.at[p // zh, sec, rows_of(p)], os_.at[d - 1], or_.at[p], sec, seq).wait_recv()
    for g in range(2):
        start(gather_copies(H, hs, hr, g))
    stage_y(W, w_sems, 0)
    wait_send(lat_copies)
    for s in range(1, ns):
        first_wait(s)
    for s in range(ns):
        merge_wait(s)
    for i in range(mid):
        proj_wait(i)
    wait_send(first_copies())

    @pl.when(composed)
    def _():
        wait_send(proj_copies())

    MD[0, y, z, c, 1] = (MD[0, y, z, c, 1].astype(F32) + MD[mid - 1, y, z, c, 0].astype(F32)).astype(BF16)
    skips[mid - 1] = jnp.zeros((2, half, SLICE), BF16)
    stage_c(W, w_sems, 0)

    def weights(s, lo, hi):
        return W[s, :, :, :, :, lo:hi].reshape(dim, hi - lo)

    def merge_weights(s, which):
        return MD[s, :, :, :, which].reshape(dim, SLICE)

    def whole(buf, g):
        return jnp.concatenate([buf[g, p] for p in range(ns)], axis=1)

    lane = lax.broadcasted_iota(jnp.int32, (half, SLICE), 1)
    pairs = [((0, 0), (0, 1))]
    near = y_order[:-1] if len(y_order) > 1 else []
    if near:
        pairs += [((near[0], 0), (near[1], 0)), ((near[0], 1), (near[1], 1))]
    pairs += [((y_order[-1], 0), (y_order[-1], 1))]

    def block(s, carry):
        par = lax.rem(s, 2)
        c_wait(W, w_sems, s)

        @pl.when((s >= 1) & (s <= mid))
        def _():
            c_wait(MD, m_sems, s - 1)

        stacked = []
        for g in range(2):
            gather_wait(H, hs, hr, g)
            total = jnp.zeros((half, SLICE), F32)
            for p in range(ns):
                total = total + H[g, p].astype(F32)
            mean = jnp.sum(total, axis=-1, keepdims=True) * (1.0 / dim)
            total = jnp.zeros((half, SLICE), F32)
            for p in range(ns):
                center = H[g, p].astype(F32) - mean
                total = total + center * center
            spread = jnp.sum(total, axis=-1, keepdims=True) * (1.0 / dim)
            inverse = lax.rsqrt(spread + EPSILON)
            normed = jnp.concatenate([((H[g, p].astype(F32) - mean) * inverse).astype(BF16) for p in range(ns)], axis=1)
            kv = jnp.dot(normed, weights(s, 128, 384), preferred_element_type=F32)
            KV[par, g, t] = kv.astype(BF16)
            start(kv_copies(par, g))
            q = jnp.dot(normed, weights(s, 0, 128), preferred_element_type=F32)
            stacked.append(jnp.concatenate([jnp.where(lane < HEAD_DIM, q, 0.0), jnp.where(lane < HEAD_DIM, 0.0, q)], axis=0).astype(BF16))

        prefetch(stage_z, s)
        for g in range(2):
            @pl.when((s >= mid - 1) & (s < ns - 1))
            def _():
                merged = jnp.dot(whole(H, g), merge_weights(s - (mid - 1), 1), preferred_element_type=F32)
                R[g] = merged + skips[ns - 2 - s, g].astype(F32)

            @pl.when((s < mid - 1) | (s == ns - 1))
            def _():
                R[g] = H[g, sec].astype(F32)

            @pl.when((s >= 1) & (s < mid))
            def _():
                skips[s - 1, g] = jnp.dot(whole(H, g), merge_weights(s - 1, 0), preferred_element_type=F32).astype(BF16)

        @pl.when((s >= 1) & (s <= mid))
        def _():
            rows = jnp.dot(WP[s - 1], merge_weights(s - 1, 1), preferred_element_type=F32)
            W[s + mid - 2, y, z, c, :, 384:512] = rows.astype(BF16)

        tops = [None, None]
        for g in range(2):
            for i, pair in enumerate(pairs):
                for d, dc in pair:
                    if (d, dc) != (0, 0):
                        kv_wait(par, g, d, dc)
                        if dc == 0:
                            relay(par, g, d).start()

                keys = jnp.concatenate([KV[par, g, kv_slot(d, dc), :, 0:SLICE] for d, dc in pair], axis=0)
                for gq in range(2):
                    scores = lax.dot_general(stacked[gq], keys, (((1,), (1,)), ((), ())), preferred_element_type=F32)
                    S[gq, g, i] = scores
                    for lo in range(0, scores.shape[1], min(SLICE, scores.shape[1])):
                        part = scores[:, lo:lo + SLICE]
                        tops[gq] = part if tops[gq] is None else jnp.maximum(tops[gq], part)
        prefetch(stage_y, s)
        for g in range(2):
            wait_send(gather_copies(H, hs, hr, g))
        for gq in range(2):
            top = jnp.max(tops[gq], axis=-1, keepdims=True)
            acc = jnp.zeros((2 * half, SLICE), F32)
            sums = None
            for g in range(2):
                for i, pair in enumerate(pairs):
                    e = jnp.exp2(S[gq, g, i] - top)
                    for lo in range(0, e.shape[1], min(SLICE, e.shape[1])):
                        part = e[:, lo:lo + SLICE]
                        sums = part if sums is None else sums + part
                    vals = jnp.concatenate([KV[par, g, kv_slot(d, dc), :, SLICE:2 * SLICE] for d, dc in pair], axis=0)
                    acc = acc + jnp.dot(e.astype(BF16), vals, preferred_element_type=F32)
            mix = acc / jnp.sum(sums, axis=-1, keepdims=True)
            A[gq, sec] = jnp.where(lane < HEAD_DIM, mix[:half], mix[half:]).astype(BF16)
            start(gather_copies(A, as_, ar, gq))
        for g in range(2):
            wait_send(kv_copies(par, g))
            wait_send([relay(par, g, d) for d in y_order])
        for g in range(2):
            gather_wait(A, as_, ar, g)
            update = jnp.dot(whole(A, g), weights(s, 384, 512), preferred_element_type=F32)
            H[g, sec] = (R[g] + update).astype(BF16)

            @pl.when(s < ns - 1)
            def _():
                start(gather_copies(H, hs, hr, g))

        prefetch(stage_c, s)
        for g in range(2):
            wait_send(gather_copies(A, as_, ar, g))
        return carry

    lax.fori_loop(0, ns, block, 0)

    out_copies = [
        rcopy(H.at[z_peer(d) // zh, sec, rows_of(z_peer(d))], O.at[z], os_.at[d - 1], or_.at[z], sec, seq_of(y, z_peer(d), c))
        for d in range(1, nz)
    ]
    start(out_copies)
    O[z] = H[z // zh, sec, local_rows(z), :]
    wait_recv([rcopy(O.at[z_peer(d)], O.at[z_peer(d)], os_.at[d - 1], or_.at[z_peer(d)], sec, seq) for d in range(1, nz)])
    out_ref[...] = O[...]
    wait_send(out_copies)


def body(latents, norm_gain, qkv_weight, proj_weight, merge_weight):
    windows, tok, dim = latents.shape
    ns = lax.axis_size("section")
    nseq = lax.axis_size("seq")
    nz = windows
    ny = nseq // (nz * CORES)
    part = dim // nseq
    sec = lax.axis_index("section")
    seq = lax.axis_index("seq")
    half = nz * tok // 2
    nt = ny * CORES
    mid = ns // 2
    lat = lax.dynamic_slice_in_dim(latents, sec * SLICE, SLICE, axis=2)
    gain = lax.dynamic_slice_in_dim(norm_gain[0], seq * part, part)[:, None]
    scale = jnp.where(jnp.arange(3 * dim) < dim, HEAD_DIM ** (-0.5) * math.log2(math.e), 1.0).astype(F32)
    folded = (qkv_weight[0].astype(F32) * gain * scale[None, :]).astype(BF16)
    packed = jnp.concatenate([folded, proj_weight[0]], axis=1)
    packed = packed.reshape(part, 4, ns, SLICE).transpose(2, 0, 1, 3).reshape(ns, part, 4 * SLICE)
    merges = merge_weight[0].reshape(part, ns, SLICE).transpose(1, 0, 2)
    dma = pltpu.SemaphoreType.DMA
    vmem = pl.BlockSpec(memory_space=pltpu.VMEM)
    gather_sems = [dma((2, ns - 1)), dma((2, ns))]
    w_sems = [dma((nz - 1,)), dma((ns, nz)), dma((ny - 1,)), dma((ns, ny)), dma((1,)), dma((ns,))]
    return pl.pallas_call(
        functools.partial(kernel, ns, ny, nz, tok),
        out_shape=jax.ShapeDtypeStruct((nz, tok, SLICE), BF16),
        in_specs=[vmem] * 4,
        out_specs=vmem,
        scratch_shapes=[
            pltpu.VMEM((2, ns, half, SLICE), BF16),
            pltpu.VMEM((2, ns, half, SLICE), BF16),
            pltpu.VMEM((2, 2, nt, half, 2 * SLICE), BF16),
            pltpu.VMEM((2, 2, nt // 2, 2 * half, 2 * half), F32),
            pltpu.VMEM((2, half, SLICE), F32),
            pltpu.VMEM((ns, ny, nz, CORES, part, 4 * SLICE), BF16),
            pltpu.VMEM((mid, ny, nz, CORES, 2, part, SLICE), BF16),
            pltpu.VMEM((mid, part, dim), BF16),
            pltpu.VMEM((mid, 2, half, SLICE), BF16),
            pltpu.VMEM((nz, tok, SLICE), BF16),
            dma((ns - 1,)), dma((ns,)),
            dma((ns - 1,)), dma((ns,)),
            dma((ns - 1,)), dma((mid,)),
            *w_sems,
            *w_sems,
            *gather_sems,
            *gather_sems,
            dma((2, ny)), dma((2, 2, nt)), dma((2, ny)),
            dma((nz - 1,)), dma((nz,)),
        ],
        compiler_params=pltpu.CompilerParams(collective_id=0, has_side_effects=True, vmem_limit_bytes=48 * 1024 * 1024),
        name="blocks",
    )(lat, packed, merges, proj_weight[0])


def solution(mesh):
    placed = (
        P(None, "seq", None),
        P("section", None),
        P("section", "seq", None),
        P("section", "seq", None),
        P("section", "seq", None),
    )
    return jax.shard_map(
        body, mesh=mesh, in_specs=placed, out_specs=P(None, "seq", "section"), check_vma=False
    )
```

```python
import functools
import math

import jax
import jax.numpy as jnp
from jax import lax
from jax.experimental import pallas as pl
from jax.experimental.pallas import tpu as pltpu
from jax.sharding import PartitionSpec as P

HEAD_DIM = 64
SLICE = 128
CORES = 2
EPSILON = 1e-05
F32 = jnp.float32
BF16 = jnp.bfloat16
MESH = pl.DeviceIdType.MESH


def rcopy(src, dst, send, recv, section, seq):
    return pltpu.make_async_remote_copy(
        src_ref=src,
        dst_ref=dst,
        send_sem=send,
        recv_sem=recv,
        device_id={"section": section, "seq": seq},
        device_id_type=MESH,
    )


def start(copies):
    for copy in copies:
        copy.start()


def wait_send(copies):
    for copy in copies:
        copy.wait_send()


def wait_recv(copies):
    for copy in copies:
        copy.wait_recv()


def kernel(ns, ny, nz, tok, lat_ref, w_ref, m_ref, p_ref, out_ref,
           H, A, KV, R, W, MD, WP, skips, O,
           p1s, p1r, m1s, m1r, q1s, q1r, wzs, wzr, wys, wyr, wcs, wcr,
           mzs, mzr, mys, myr, mcs, mcr, hs, hr, as_, ar, kvs, kvr, kvx, rls, os_, or_):
    nc = CORES
    mid = ns // 2
    dim = ns * SLICE
    zh = nz // 2
    half = zh * tok
    sec = lax.axis_index("section")
    seq = lax.axis_index("seq")
    y = seq // (nz * nc)
    z = (seq // nc) % nz
    c = seq % nc

    def seq_of(y_, z_, c_):
        return y_ * (nz * nc) + z_ * nc + c_

    nx = ns // 2
    farthest = [(dx, dz) for dx in range(nx) for dz in range(2) if (dx, dz) != (0, 0)]
    farthest.sort(key=lambda o: -(min(o[0], nx - o[0]) + o[1]))

    def sec_peer(d):
        dx, dz = farthest[d - 1]
        return lax.rem(sec // nx + dz, 2) * nx + lax.rem(sec + dx, nx)

    def z_peer(d):
        return lax.rem(z + d, nz)

    def y_peer(d):
        return lax.rem(y + d, ny)

    y_order = sorted(range(1, ny), key=lambda d: -min(d, ny - d))
    sibling = seq_of(y, z, 1 - c)

    barrier = pltpu.get_barrier_semaphore()
    greeted = [(sec_peer(d), seq) for d in range(1, ns)]
    greeted += [(sec, seq_of(y, z_peer(d), c)) for d in range(1, nz)]
    greeted += [(sec, seq_of(y_peer(d), z, c)) for d in range(1, ny)]
    greeted += [(sec, sibling)]
    for section_, seq_ in greeted:
        pl.semaphore_signal(barrier, inc=1, device_id={"section": section_, "seq": seq_}, device_id_type=MESH)
    pl.semaphore_wait(barrier, len(greeted))

    def first_copies():
        return [rcopy(w_ref.at[sec_peer(d)], W.at[sec, y, z, c], p1s.at[d - 1], p1r.at[sec], sec_peer(d), seq) for d in range(1, ns)]

    def merge_copies():
        return [
            rcopy(m_ref.at[sec_peer(d)], MD.at[sec % mid, y, z, c, sec // mid], m1s.at[d - 1], m1r.at[sec], sec_peer(d), seq)
            for d in range(1, ns)
        ]

    def first_wait(s):
        @pl.when(sec != s)
        def _():
            rcopy(w_ref.at[s], W.at[s, y, z, c], p1s.at[0], p1r.at[s], sec, seq).wait_recv()

    def merge_wait(s):
        @pl.when(sec != s)
        def _():
            rcopy(m_ref.at[s], MD.at[s % mid, y, z, c, s // mid], m1s.at[0], m1r.at[s], sec, seq).wait_recv()

    composed = (sec >= mid - 1) & (sec < ns - 1)

    def proj_copies():
        return [rcopy(p_ref, WP.at[sec - (mid - 1)], q1s.at[d - 1], q1r.at[sec - (mid - 1)], sec_peer(d), seq) for d in range(1, ns)]

    def proj_wait(i):
        @pl.when(sec != i + mid - 1)
        def _():
            rcopy(p_ref, WP.at[i], q1s.at[0], q1r.at[i], sec, seq).wait_recv()

    w_sems = (wzs, wzr, wys, wyr, wcs, wcr)
    m_sems = (mzs, mzr, mys, myr, mcs, mcr)

    def z_copies(ref, sems, s):
        return [rcopy(ref.at[s, y, z, c], ref.at[s, y, z, c], sems[0].at[0], sems[1].at[s], sec, seq_of(y, z_peer(d), c)) for d in range(1, nz)]

    def z_all(ref, sems, s):
        part = ref.at[s, y, pl.ds(0, nz - 1), c]
        return rcopy(part, part, sems[0].at[0], sems[1].at[s], sec, sibling)

    def y_copies(ref, sems, s):
        return [rcopy(ref.at[s, y, :, c], ref.at[s, y, :, c], sems[2].at[0], sems[3].at[s], sec, seq_of(y_peer(d), z, c)) for d in y_order]

    def y_all(ref, sems, s):
        part = ref.at[s, pl.ds(0, ny - 1), :, c]
        return rcopy(part, part, sems[2].at[0], sems[3].at[s], sec, sibling)

    def c_copy(ref, sems, s):
        return rcopy(ref.at[s, :, :, c], ref.at[s, :, :, c], sems[4].at[0], sems[5].at[s], sec, sibling)

    def c_wait(ref, sems, s):
        c_copy(ref, sems, s).wait_send()
        rcopy(ref.at[s, :, :, 1 - c], ref.at[s, :, :, 1 - c], sems[4].at[0], sems[5].at[s], sec, seq).wait_recv()

    def stage_z(ref, sems, s):
        start(z_copies(ref, sems, s))

    def stage_y(ref, sems, s):
        z_all(ref, sems, s).wait_recv()
        start(y_copies(ref, sems, s))
        z_all(ref, sems, s).wait_send()

    def stage_c(ref, sems, s):
        y_all(ref, sems, s).wait_recv()
        c_copy(ref, sems, s).start()
        y_all(ref, sems, s).wait_send()

    def prefetch(stage, s):
        @pl.when(s < ns - 1)
        def _():
            stage(W, w_sems, s + 1)

        @pl.when(s < mid)
        def _():
            stage(MD, m_sems, s)

    def gather_start(buf, ssem, rsem, g):
        start([rcopy(buf.at[g, sec], buf.at[g, sec], ssem.at[g], rsem.at[g], sec_peer(d), seq) for d in range(1, ns)])

    def gather_all(buf, ssem, rsem, g):
        part = buf.at[g, pl.ds(0, ns - 1)]
        return rcopy(part, part, ssem.at[g], rsem.at[g], sec, sibling)

    def kv_start(par, g):
        own = KV.at[par, g, c, y]
        start([rcopy(own, own, kvs.at[g], kvr.at[par, g, y], sec, seq_of(y_peer(d), z, c)) for d in y_order])
        rcopy(own, own, kvs.at[g], kvx.at[par, g], sec, sibling).start()

    def kv_sent(par, g):
        part = KV.at[par, g, c, pl.ds(0, ny)]
        rcopy(part, part, kvs.at[g], kvx.at[par, g], sec, sibling).wait_send()
        part = KV.at[par, g, c, pl.ds(0, ny - 1)]
        rcopy(part, part, rls.at[g], kvx.at[par, g], sec, sibling).wait_send()

    def kv_relay(par, g, d):
        p = y_peer(d)
        slot = KV.at[par, g, c, p]
        rcopy(slot, slot, rls.at[g], kvr.at[par, g, p], sec, sibling).wait_recv()
        rcopy(slot, slot, rls.at[g], kvx.at[par, g], sec, sibling).start()

    def kv_other(par, g):
        part = KV.at[par, g, 1 - c, pl.ds(0, ny)]
        rcopy(part, part, kvs.at[g], kvx.at[par, g], sec, sibling).wait_recv()

    def rows_of(z_):
        return pl.ds(lax.rem(z_, zh) * tok, tok)

    def local_rows(z_):
        return pl.ds(pl.multiple_of(lax.rem(z_, zh) * tok, tok), tok)

    @pl.when(sec == 0)
    def _():
        start(first_copies())

    lat_copies = [
        rcopy(lat_ref.at[z_peer(d)], H.at[z // zh, sec, rows_of(z)], os_.at[d - 1], or_.at[z], sec, seq_of(y, z_peer(d), c))
        for d in range(1, nz)
    ]
    start(lat_copies)
    W[sec, y, z, c] = w_ref[sec]
    MD[sec % mid, y, z, c, sec // mid] = m_ref[sec]
    H[z // zh, sec, local_rows(z), :] = lat_ref[z]

    @pl.when(composed)
    def _():
        WP[sec - (mid - 1)] = p_ref[...]

    first_wait(0)
    stage_z(W, w_sems, 0)
    for d in range(1, nz):
        p = z_peer(d)
        rcopy(lat_ref.at[p], H.at[p // zh, sec, rows_of(p)], os_.at[d - 1], or_.at[p], sec, seq).wait_recv()
    for g in range(2):
        gather_start(H, hs, hr, g)
    stage_y(W, w_sems, 0)

    @pl.when(sec != 0)
    def _():
        start(first_copies())

    start(merge_copies())
    wait_send(lat_copies)
    skips[mid - 1] = jnp.zeros((2, half, SLICE), BF16)
    stage_c(W, w_sems, 0)

    @pl.when(composed)
    def _():
        start(proj_copies())

    for s in range(1, ns):
        first_wait(s)
    for s in range(ns):
        merge_wait(s)
    wait_send(first_copies())
    wait_send(merge_copies())
    MD[0, y, z, c, 1] = (MD[0, y, z, c, 1].astype(F32) + MD[mid - 1, y, z, c, 0].astype(F32)).astype(BF16)

    def weights(s, lo, hi):
        return W[s, :, :, :, :, lo:hi].reshape(dim, hi - lo)

    def merge_weights(s, which):
        return MD[s, :, :, :, which].reshape(dim, SLICE)

    def whole(buf, g):
        return jnp.concatenate([buf[g, p] for p in range(ns)], axis=1)

    lane = lax.broadcasted_iota(jnp.int32, (half, SLICE), 1)
    def block(s, carry):
        par = lax.rem(s, 2)
        c_wait(W, w_sems, s)

        @pl.when((s >= 1) & (s <= mid))
        def _():
            c_wait(MD, m_sems, s - 1)

        stacked = []
        for g in range(2):
            gather_all(H, hs, hr, g).wait_recv()
            total = jnp.zeros((half, SLICE), F32)
            for p in range(ns):
                total = total + H[g, p].astype(F32)
            mean = jnp.sum(total, axis=-1, keepdims=True) * (1.0 / dim)
            total = jnp.zeros((half, SLICE), F32)
            for p in range(ns):
                center = H[g, p].astype(F32) - mean
                total = total + center * center
            spread = jnp.sum(total, axis=-1, keepdims=True) * (1.0 / dim)
            inverse = lax.rsqrt(spread + EPSILON)
            normed = jnp.concatenate([((H[g, p].astype(F32) - mean) * inverse).astype(BF16) for p in range(ns)], axis=1)
            kv = jnp.dot(normed, weights(s, 128, 384), preferred_element_type=F32)
            KV[par, g, c, y] = kv.astype(BF16)
            kv_start(par, g)
            q = jnp.dot(normed, weights(s, 0, 128), preferred_element_type=F32)
            stacked.append(jnp.concatenate([jnp.where(lane < HEAD_DIM, q, 0.0), jnp.where(lane < HEAD_DIM, 0.0, q)], axis=0).astype(BF16))

        prefetch(stage_z, s)
        for g in range(2):
            @pl.when((s >= mid - 1) & (s < ns - 1))
            def _():
                merged = jnp.dot(whole(H, g), merge_weights(s - (mid - 1), 1), preferred_element_type=F32)
                R[g] = merged + skips[ns - 2 - s, g].astype(F32)

            @pl.when((s < mid - 1) | (s == ns - 1))
            def _():
                R[g] = H[g, sec].astype(F32)

            @pl.when((s >= 1) & (s < mid))
            def _():
                skips[s - 1, g] = jnp.dot(whole(H, g), merge_weights(s - 1, 0), preferred_element_type=F32).astype(BF16)

        @pl.when((s >= 1) & (s <= mid))
        def _():
            rows = jnp.dot(WP[s - 1], merge_weights(s - 1, 1), preferred_element_type=F32)
            W[s + mid - 2, y, z, c, :, 384:512] = rows.astype(BF16)

        tops, sums, mixes = [None, None], [None, None], [None, None]

        def attend(gq, g, core):
            keys = KV[par, g, core, :, :, 0:SLICE].reshape(ny * half, SLICE)
            vals = KV[par, g, core, :, :, SLICE:2 * SLICE].reshape(ny * half, SLICE)
            scores = lax.dot_general(stacked[gq], keys, (((1,), (1,)), ((), ())), preferred_element_type=F32)
            top = jnp.max(scores, axis=-1, keepdims=True)
            if tops[gq] is not None:
                top = jnp.maximum(tops[gq], top)
            e = jnp.exp2(scores - top)
            mix = jnp.dot(e.astype(BF16), vals, preferred_element_type=F32)
            total = jnp.sum(e, axis=-1, keepdims=True)
            if tops[gq] is not None:
                fade = jnp.exp2(tops[gq] - top)
                mix = mixes[gq] * fade + mix
                total = sums[gq] * fade + total
            tops[gq], sums[gq], mixes[gq] = top, total, mix

        for g in range(2):
            for d in reversed(y_order):
                kv_relay(par, g, d)
            for gq in range(2):
                attend(gq, g, c)
            if g == 1:
                prefetch(stage_y, s)
                for half_ in range(2):
                    gather_all(H, hs, hr, half_).wait_send()
            kv_other(par, g)
            for gq in range(2):
                attend(gq, g, 1 - c)
                if g == 1:
                    mix = mixes[gq] / sums[gq]
                    A[gq, sec] = jnp.where(lane < HEAD_DIM, mix[:half], mix[half:]).astype(BF16)
                    gather_start(A, as_, ar, gq)
        for g in range(2):
            kv_sent(par, g)

        @pl.when(s == 0)
        def _():
            for i in range(mid):
                proj_wait(i)

        @pl.when((s == 0) & composed)
        def _():
            wait_send(proj_copies())

        for g in range(2):
            gather_all(A, as_, ar, g).wait_recv()
            update = jnp.dot(whole(A, g), weights(s, 384, 512), preferred_element_type=F32)
            H[g, sec] = (R[g] + update).astype(BF16)

            @pl.when(s < ns - 1)
            def _():
                gather_start(H, hs, hr, g)

        prefetch(stage_c, s)
        for g in range(2):
            gather_all(A, as_, ar, g).wait_send()
        return carry

    lax.fori_loop(0, ns, block, 0)

    out_copies = [
        rcopy(H.at[z_peer(d) // zh, sec, rows_of(z_peer(d))], O.at[z], os_.at[d - 1], or_.at[z], sec, seq_of(y, z_peer(d), c))
        for d in range(1, nz)
    ]
    start(out_copies)
    O[z] = H[z // zh, sec, local_rows(z), :]
    wait_recv([rcopy(O.at[z_peer(d)], O.at[z_peer(d)], os_.at[d - 1], or_.at[z_peer(d)], sec, seq) for d in range(1, nz)])
    out_ref[...] = O[...]
    wait_send(out_copies)


def body(latents, norm_gain, qkv_weight, proj_weight, merge_weight):
    windows, tok, dim = latents.shape
    ns = lax.axis_size("section")
    nseq = lax.axis_size("seq")
    nz = windows
    ny = nseq // (nz * CORES)
    part = dim // nseq
    sec = lax.axis_index("section")
    seq = lax.axis_index("seq")
    half = nz * tok // 2
    mid = ns // 2
    lat = lax.dynamic_slice_in_dim(latents, sec * SLICE, SLICE, axis=2)
    gain = lax.dynamic_slice_in_dim(norm_gain[0], seq * part, part)[:, None]
    scale = jnp.where(jnp.arange(3 * dim) < dim, HEAD_DIM ** (-0.5) * math.log2(math.e), 1.0).astype(F32)
    folded = (qkv_weight[0].astype(F32) * gain * scale[None, :]).astype(BF16)
    packed = jnp.concatenate([folded, proj_weight[0]], axis=1)
    packed = packed.reshape(part, 4, ns, SLICE).transpose(2, 0, 1, 3).reshape(ns, part, 4 * SLICE)
    merges = merge_weight[0].reshape(part, ns, SLICE).transpose(1, 0, 2)
    dma = pltpu.SemaphoreType.DMA
    vmem = pl.BlockSpec(memory_space=pltpu.VMEM)
    gather_sems = [dma((2,)), dma((2,))]
    w_sems = [dma((1,)), dma((ns,)), dma((1,)), dma((ns,)), dma((1,)), dma((ns,))]
    return pl.pallas_call(
        functools.partial(kernel, ns, ny, nz, tok),
        out_shape=jax.ShapeDtypeStruct((nz, tok, SLICE), BF16),
        in_specs=[vmem] * 4,
        out_specs=vmem,
        scratch_shapes=[
            pltpu.VMEM((2, ns, half, SLICE), BF16),
            pltpu.VMEM((2, ns, half, SLICE), BF16),
            pltpu.VMEM((2, 2, CORES, ny, half, 2 * SLICE), BF16),
            pltpu.VMEM((2, half, SLICE), F32),
            pltpu.VMEM((ns, ny, nz, CORES, part, 4 * SLICE), BF16),
            pltpu.VMEM((mid, ny, nz, CORES, 2, part, SLICE), BF16),
            pltpu.VMEM((mid, part, dim), BF16),
            pltpu.VMEM((mid, 2, half, SLICE), BF16),
            pltpu.VMEM((nz, tok, SLICE), BF16),
            dma((ns - 1,)), dma((ns,)),
            dma((ns - 1,)), dma((ns,)),
            dma((ns - 1,)), dma((mid,)),
            *w_sems,
            *w_sems,
            *gather_sems,
            *gather_sems,
            dma((2,)), dma((2, 2, ny)), dma((2, 2)), dma((2,)),
            dma((nz - 1,)), dma((nz,)),
        ],
        compiler_params=pltpu.CompilerParams(collective_id=0, has_side_effects=True, vmem_limit_bytes=48 * 1024 * 1024),
        name="blocks",
    )(lat, packed, merges, proj_weight[0])


def solution(mesh):
    placed = (
        P(None, "seq", None),
        P("section", None),
        P("section", "seq", None),
        P("section", "seq", None),
        P("section", "seq", None),
    )
    return jax.shard_map(
        body, mesh=mesh, in_specs=placed, out_specs=P(None, "seq", "section"), check_vma=False
    )
```

```python
import functools
import math

import jax
import jax.numpy as jnp
from jax import lax
from jax.experimental import pallas as pl
from jax.experimental.pallas import tpu as pltpu
from jax.sharding import PartitionSpec as P

HEAD_DIM = 64
SLICE = 128
CORES = 2
EPSILON = 1e-05
F32 = jnp.float32
BF16 = jnp.bfloat16
MESH = pl.DeviceIdType.MESH


def rcopy(src, dst, send, recv, section, seq):
    return pltpu.make_async_remote_copy(
        src_ref=src,
        dst_ref=dst,
        send_sem=send,
        recv_sem=recv,
        device_id={"section": section, "seq": seq},
        device_id_type=MESH,
    )


def start(copies):
    for copy in copies:
        copy.start()


def wait_send(copies):
    for copy in copies:
        copy.wait_send()


def wait_recv(copies):
    for copy in copies:
        copy.wait_recv()


def kernel(ns, ny, nz, tok, lat_hbm, gain_hbm, qkv_hbm, p_hbm, merge_hbm, out_ref,
           lat_ref, gain_ref, qkv_ref, p_ref, merge_ref, in_sems, w_ref, m_ref, H, A, KV, R, W, MD, WP, skips, O,
           p1s, p1r, m1s, m1r, q1s, q1r, z0r, wzs, wzr, wys, wyr, wcs, wcr,
           mzs, mzr, mys, myr, mcs, mcr, hs, hr, as_, ar, kvs, kvr, kvx, rls, os_, or_):
    nc = CORES
    mid = ns // 2
    dim = ns * SLICE
    zh = nz // 2
    half = zh * tok
    sec = lax.axis_index("section")
    seq = lax.axis_index("seq")
    y = seq // (nz * nc)
    z = (seq // nc) % nz
    c = seq % nc

    def seq_of(y_, z_, c_):
        return y_ * (nz * nc) + z_ * nc + c_

    nx = ns // 2
    farthest = [(dx, dz) for dx in range(nx) for dz in range(2) if (dx, dz) != (0, 0)]
    farthest.sort(key=lambda o: -(min(o[0], nx - o[0]) + o[1]))

    def sec_peer(d):
        dx, dz = farthest[d - 1]
        return lax.rem(sec // nx + dz, 2) * nx + lax.rem(sec + dx, nx)

    def z_peer(d):
        return lax.rem(z + d, nz)

    def y_peer(d):
        return lax.rem(y + d, ny)

    y_order = sorted(range(1, ny), key=lambda d: -min(d, ny - d))
    sibling = seq_of(y, z, 1 - c)

    columns = pl.ds(pl.multiple_of(sec * SLICE, SLICE), SLICE)
    loads = [
        pltpu.make_async_copy(src, dst, in_sems.at[i])
        for i, (src, dst) in enumerate([
            (qkv_hbm, qkv_ref), (gain_hbm, gain_ref), (p_hbm, p_ref), (merge_hbm, merge_ref), (lat_hbm.at[:, :, columns], lat_ref)])
    ]
    start(loads)
    barrier = pltpu.get_barrier_semaphore()
    greeted = [(sec_peer(d), seq) for d in range(1, ns)]
    greeted += [(sec, seq_of(y, z_peer(d), c)) for d in range(1, nz)]
    greeted += [(sec, seq_of(y_peer(d), z, c)) for d in range(1, ny)]
    greeted += [(sec, sibling)]
    for section_, seq_ in greeted:
        pl.semaphore_signal(barrier, inc=1, device_id={"section": section_, "seq": seq_}, device_id_type=MESH)

    for load in loads:
        load.wait()
    part = qkv_ref.shape[0]
    places = lax.broadcasted_iota(jnp.int32, (part, dim), 1) - lax.broadcasted_iota(jnp.int32, (part, dim), 0)
    gain = jnp.sum(jnp.where(places == seq * part, gain_ref[...], 0.0), axis=-1, keepdims=True)
    for j in range(ns):
        for k in range(3):
            at = k * dim + j * SLICE
            piece = qkv_ref[:, at:at + SLICE].astype(F32) * gain
            if k == 0:
                piece = piece * (HEAD_DIM ** (-0.5) * math.log2(math.e))
            w_ref[j, :, k * SLICE:(k + 1) * SLICE] = piece.astype(BF16)
        w_ref[j, :, 3 * SLICE:] = p_ref[:, j * SLICE:(j + 1) * SLICE]
        m_ref[j] = merge_ref[:, j * SLICE:(j + 1) * SLICE]
    pl.semaphore_wait(barrier, len(greeted))

    def first_copies():
        return [rcopy(w_ref.at[sec_peer(d)], W.at[sec, y, z, c], p1s.at[d - 1], p1r.at[sec], sec_peer(d), seq) for d in range(1, ns)]

    def merge_copies():
        return [
            rcopy(m_ref.at[sec_peer(d)], MD.at[sec % mid, y, z, c, sec // mid], m1s.at[d - 1], m1r.at[sec], sec_peer(d), seq)
            for d in range(1, ns)
        ]

    def first_wait(s):
        @pl.when(sec != s)
        def _():
            rcopy(w_ref.at[s], W.at[s, y, z, c], p1s.at[0], p1r.at[s], sec, seq).wait_recv()

    def merge_wait(s):
        @pl.when(sec != s)
        def _():
            rcopy(m_ref.at[s], MD.at[s % mid, y, z, c, s // mid], m1s.at[0], m1r.at[s], sec, seq).wait_recv()

    composed = (sec >= mid - 1) & (sec < ns - 1)

    def proj_copies():
        return [rcopy(p_ref, WP.at[sec - (mid - 1)], q1s.at[d - 1], q1r.at[sec - (mid - 1)], sec_peer(d), seq) for d in range(1, ns)]

    def proj_wait(i):
        @pl.when(sec != i + mid - 1)
        def _():
            rcopy(p_ref, WP.at[i], q1s.at[0], q1r.at[i], sec, seq).wait_recv()

    w_sems = (wzs, wzr, wys, wyr, wcs, wcr)
    m_sems = (mzs, mzr, mys, myr, mcs, mcr)

    def z_copies(ref, sems, s):
        return [rcopy(ref.at[s, y, z, c], ref.at[s, y, z, c], sems[0].at[0], sems[1].at[s], sec, seq_of(y, z_peer(d), c)) for d in range(1, nz)]

    def z_all(ref, sems, s):
        part = ref.at[s, y, pl.ds(0, nz - 1), c]
        return rcopy(part, part, sems[0].at[0], sems[1].at[s], sec, sibling)

    def y_copies(ref, sems, s):
        return [rcopy(ref.at[s, y, :, c], ref.at[s, y, :, c], sems[2].at[0], sems[3].at[s], sec, seq_of(y_peer(d), z, c)) for d in y_order]

    def y_all(ref, sems, s):
        part = ref.at[s, pl.ds(0, ny - 1), :, c]
        return rcopy(part, part, sems[2].at[0], sems[3].at[s], sec, sibling)

    def c_copy(ref, sems, s):
        return rcopy(ref.at[s, :, :, c], ref.at[s, :, :, c], sems[4].at[0], sems[5].at[s], sec, sibling)

    def c_wait(ref, sems, s):
        c_copy(ref, sems, s).wait_send()
        rcopy(ref.at[s, :, :, 1 - c], ref.at[s, :, :, 1 - c], sems[4].at[0], sems[5].at[s], sec, seq).wait_recv()

    def stage_z(ref, sems, s):
        start(z_copies(ref, sems, s))

    def stage_y(ref, sems, s):
        z_all(ref, sems, s).wait_recv()
        start(y_copies(ref, sems, s))
        z_all(ref, sems, s).wait_send()

    def stage_c(ref, sems, s):
        y_all(ref, sems, s).wait_recv()
        c_copy(ref, sems, s).start()
        y_all(ref, sems, s).wait_send()

    def prefetch(stage, s):
        @pl.when(s < ns - 1)
        def _():
            stage(W, w_sems, s + 1)

        @pl.when(s < mid)
        def _():
            stage(MD, m_sems, s)

    def prefetch_z(s):
        @pl.when(s < ns - 1)
        def _():
            @pl.when((s + 1 < mid - 1) | (s + 1 == ns - 1))
            def _():
                first_wait(s + 1)

            stage_z(W, w_sems, s + 1)

        @pl.when(s < mid)
        def _():
            @pl.when(s < mid - 1)
            def _():
                merge_wait(s)

            merge_wait(s + mid)

            @pl.when(s == 0)
            def _():
                merge_wait(mid - 1)
                MD[0, y, z, c, 1] = (MD[0, y, z, c, 1].astype(F32) + MD[mid - 1, y, z, c, 0].astype(F32)).astype(BF16)

            stage_z(MD, m_sems, s)

    def gather_start(buf, ssem, rsem, g):
        start([rcopy(buf.at[g, sec], buf.at[g, sec], ssem.at[g], rsem.at[g], sec_peer(d), seq) for d in range(1, ns)])

    def gather_all(buf, ssem, rsem, g):
        part = buf.at[g, pl.ds(0, ns - 1)]
        return rcopy(part, part, ssem.at[g], rsem.at[g], sec, sibling)

    def kv_start(par, g):
        own = KV.at[par, g, c, y]
        start([rcopy(own, own, kvs.at[g], kvr.at[par, g, y], sec, seq_of(y_peer(d), z, c)) for d in y_order])
        rcopy(own, own, kvs.at[g], kvx.at[par, g], sec, sibling).start()

    def kv_sent(par, g):
        part = KV.at[par, g, c, pl.ds(0, ny)]
        rcopy(part, part, kvs.at[g], kvx.at[par, g], sec, sibling).wait_send()
        part = KV.at[par, g, c, pl.ds(0, ny - 1)]
        rcopy(part, part, rls.at[g], kvx.at[par, g], sec, sibling).wait_send()

    def kv_relay(par, g, d):
        p = y_peer(d)
        slot = KV.at[par, g, c, p]
        rcopy(slot, slot, rls.at[g], kvr.at[par, g, p], sec, sibling).wait_recv()
        rcopy(slot, slot, rls.at[g], kvx.at[par, g], sec, sibling).start()

    def kv_other(par, g):
        part = KV.at[par, g, 1 - c, pl.ds(0, ny)]
        rcopy(part, part, kvs.at[g], kvx.at[par, g], sec, sibling).wait_recv()

    def rows_of(z_):
        return pl.ds(lax.rem(z_, zh) * tok, tok)

    def local_rows(z_):
        return pl.ds(pl.multiple_of(lax.rem(z_, zh) * tok, tok), tok)

    @pl.when(sec == 0)
    def _():
        start(first_copies())

    lat_copies = [
        rcopy(lat_ref.at[z_peer(d)], H.at[z // zh, sec, rows_of(z)], os_.at[d - 1], or_.at[z], sec, seq_of(y, z_peer(d), c))
        for d in range(1, nz)
    ]
    start(lat_copies)
    W[sec, y, z, c] = w_ref[sec]
    MD[sec % mid, y, z, c, sec // mid] = m_ref[sec]
    H[z // zh, sec, local_rows(z), :] = lat_ref[z]

    @pl.when(composed)
    def _():
        WP[sec - (mid - 1)] = p_ref[...]

    first_wait(0)

    def along_y(z_):
        return [rcopy(W.at[0, y, z_, c], W.at[0, y, z_, c], wys.at[0], wyr.at[0], sec, seq_of(y_peer(d), z, c)) for d in y_order]

    start([rcopy(W.at[0, y, z, c], W.at[0, y, z, c], wzs.at[0], z0r.at[z], sec, seq_of(y, z_peer(d), c)) for d in range(1, nz)])
    start(along_y(z))
    for d in range(1, nz):
        p = z_peer(d)
        rcopy(lat_ref.at[p], H.at[p // zh, sec, rows_of(p)], os_.at[d - 1], or_.at[p], sec, seq).wait_recv()
    gather_start(H, hs, hr, 0)
    for d in sorted(range(1, nz), key=lambda d: min(d, nz - d)):
        p = z_peer(d)
        rcopy(W.at[0, y, p, c], W.at[0, y, p, c], wzs.at[0], z0r.at[p], sec, seq).wait_recv()
        start(along_y(p))
    gather_start(H, hs, hr, 1)

    @pl.when(sec != 0)
    def _():
        start(first_copies())

    start(merge_copies())
    z_all(W, w_sems, 0).wait_send()
    wait_send(lat_copies)
    skips[mid - 1] = jnp.zeros((2, half, SLICE), BF16)
    stage_c(W, w_sems, 0)

    def weights(s, lo, hi):
        return W[s, :, :, :, :, lo:hi].reshape(dim, hi - lo)

    def merge_weights(s, which):
        return MD[s, :, :, :, which].reshape(dim, SLICE)

    def whole(buf, g):
        return jnp.concatenate([buf[g, p] for p in range(ns)], axis=1)

    lane = lax.broadcasted_iota(jnp.int32, (half, SLICE), 1)
    def block(s, carry):
        par = lax.rem(s, 2)
        c_wait(W, w_sems, s)

        @pl.when((s >= 1) & (s <= mid))
        def _():
            c_wait(MD, m_sems, s - 1)

        stacked = []
        for g in range(2):
            gather_all(H, hs, hr, g).wait_recv()
            total = jnp.zeros((half, SLICE), F32)
            for p in range(ns):
                total = total + H[g, p].astype(F32)
            mean = jnp.sum(total, axis=-1, keepdims=True) * (1.0 / dim)
            total = jnp.zeros((half, SLICE), F32)
            for p in range(ns):
                center = H[g, p].astype(F32) - mean
                total = total + center * center
            spread = jnp.sum(total, axis=-1, keepdims=True) * (1.0 / dim)
            inverse = lax.rsqrt(spread + EPSILON)
            normed = jnp.concatenate([((H[g, p].astype(F32) - mean) * inverse).astype(BF16) for p in range(ns)], axis=1)
            kv = jnp.dot(normed, weights(s, 128, 384), preferred_element_type=F32)
            KV[par, g, c, y] = kv.astype(BF16)
            kv_start(par, g)
            q = jnp.dot(normed, weights(s, 0, 128), preferred_element_type=F32)
            stacked.append(jnp.concatenate([jnp.where(lane < HEAD_DIM, q, 0.0), jnp.where(lane < HEAD_DIM, 0.0, q)], axis=0).astype(BF16))

        prefetch_z(s)

        @pl.when((s == 0) & composed)
        def _():
            start(proj_copies())

        for g in range(2):
            @pl.when((s >= mid - 1) & (s < ns - 1))
            def _():
                merged = jnp.dot(whole(H, g), merge_weights(s - (mid - 1), 1), preferred_element_type=F32)
                R[g] = merged + skips[ns - 2 - s, g].astype(F32)

            @pl.when((s < mid - 1) | (s == ns - 1))
            def _():
                R[g] = H[g, sec].astype(F32)

            @pl.when((s >= 1) & (s < mid))
            def _():
                skips[s - 1, g] = jnp.dot(whole(H, g), merge_weights(s - 1, 0), preferred_element_type=F32).astype(BF16)

        @pl.when(s == 1)
        def _():
            for i in range(mid):
                proj_wait(i)

            @pl.when(composed)
            def _():
                wait_send(proj_copies())

        @pl.when((s >= 1) & (s <= mid))
        def _():
            first_wait(s + mid - 2)
            rows = jnp.dot(WP[s - 1], merge_weights(s - 1, 1), preferred_element_type=F32)
            W[s + mid - 2, y, z, c, :, 384:512] = rows.astype(BF16)

        tops, sums, mixes = [None, None], [None, None], [None, None]

        def attend(gq, g, core):
            keys = KV[par, g, core, :, :, 0:SLICE].reshape(ny * half, SLICE)
            vals = KV[par, g, core, :, :, SLICE:2 * SLICE].reshape(ny * half, SLICE)
            scores = lax.dot_general(stacked[gq], keys, (((1,), (1,)), ((), ())), preferred_element_type=F32)
            top = jnp.max(scores, axis=-1, keepdims=True)
            if tops[gq] is not None:
                top = jnp.maximum(tops[gq], top)
            e = jnp.exp2(scores - top)
            mix = jnp.dot(e.astype(BF16), vals, preferred_element_type=F32)
            total = jnp.sum(e, axis=-1, keepdims=True)
            if tops[gq] is not None:
                fade = jnp.exp2(tops[gq] - top)
                mix = mixes[gq] * fade + mix
                total = sums[gq] * fade + total
            tops[gq], sums[gq], mixes[gq] = top, total, mix

        for g in range(2):
            for d in reversed(y_order):
                kv_relay(par, g, d)
            for gq in range(2):
                attend(gq, g, c)
            if g == 1:
                prefetch(stage_y, s)
                for half_ in range(2):
                    gather_all(H, hs, hr, half_).wait_send()
            kv_other(par, g)
            for gq in range(2):
                attend(gq, g, 1 - c)
                if g == 1:
                    mix = mixes[gq] / sums[gq]
                    A[gq, sec] = jnp.where(lane < HEAD_DIM, mix[:half], mix[half:]).astype(BF16)
                    gather_start(A, as_, ar, gq)
        for g in range(2):
            kv_sent(par, g)

        for g in range(2):
            gather_all(A, as_, ar, g).wait_recv()
            update = jnp.dot(whole(A, g), weights(s, 384, 512), preferred_element_type=F32)
            H[g, sec] = (R[g] + update).astype(BF16)

            @pl.when(s < ns - 1)
            def _():
                gather_start(H, hs, hr, g)

        prefetch(stage_c, s)
        for g in range(2):
            gather_all(A, as_, ar, g).wait_send()
        return carry

    lax.fori_loop(0, ns, block, 0)

    out_copies = [
        rcopy(H.at[z_peer(d) // zh, sec, rows_of(z_peer(d))], O.at[z], os_.at[d - 1], or_.at[z], sec, seq_of(y, z_peer(d), c))
        for d in range(1, nz)
    ]
    start(out_copies)
    O[z] = H[z // zh, sec, local_rows(z), :]
    wait_recv([rcopy(O.at[z_peer(d)], O.at[z_peer(d)], os_.at[d - 1], or_.at[z_peer(d)], sec, seq) for d in range(1, nz)])
    out_ref[...] = O[...]
    wait_send(first_copies())
    wait_send(merge_copies())
    wait_send(out_copies)


def body(latents, norm_gain, qkv_weight, proj_weight, merge_weight):
    windows, tok, dim = latents.shape
    ns = lax.axis_size("section")
    nseq = lax.axis_size("seq")
    nz = windows
    ny = nseq // (nz * CORES)
    part = dim // nseq
    half = nz * tok // 2
    mid = ns // 2
    dma = pltpu.SemaphoreType.DMA
    vmem = pl.BlockSpec(memory_space=pltpu.VMEM)
    gather_sems = [dma((2,)), dma((2,))]
    w_sems = [dma((1,)), dma((ns,)), dma((1,)), dma((ns,)), dma((1,)), dma((ns,))]
    return pl.pallas_call(
        functools.partial(kernel, ns, ny, nz, tok),
        out_shape=jax.ShapeDtypeStruct((nz, tok, SLICE), BF16),
        in_specs=[pl.BlockSpec(memory_space=pltpu.MemorySpace.HBM)] * 5,
        out_specs=vmem,
        scratch_shapes=[
            pltpu.VMEM((nz, tok, SLICE), BF16),
            pltpu.VMEM((1, dim), F32),
            pltpu.VMEM((part, 3 * dim), BF16),
            pltpu.VMEM((part, dim), BF16),
            pltpu.VMEM((part, dim), BF16),
            dma((5,)),
            pltpu.VMEM((ns, part, 4 * SLICE), BF16),
            pltpu.VMEM((ns, part, SLICE), BF16),
            pltpu.VMEM((2, ns, half, SLICE), BF16),
            pltpu.VMEM((2, ns, half, SLICE), BF16),
            pltpu.VMEM((2, 2, CORES, ny, half, 2 * SLICE), BF16),
            pltpu.VMEM((2, half, SLICE), F32),
            pltpu.VMEM((ns, ny, nz, CORES, part, 4 * SLICE), BF16),
            pltpu.VMEM((mid, ny, nz, CORES, 2, part, SLICE), BF16),
            pltpu.VMEM((mid, part, dim), BF16),
            pltpu.VMEM((mid, 2, half, SLICE), BF16),
            pltpu.VMEM((nz, tok, SLICE), BF16),
            dma((ns - 1,)), dma((ns,)),
            dma((ns - 1,)), dma((ns,)),
            dma((ns - 1,)), dma((mid,)),
            dma((nz,)),
            *w_sems,
            *w_sems,
            *gather_sems,
            *gather_sems,
            dma((2,)), dma((2, 2, ny)), dma((2, 2)), dma((2,)),
            dma((nz - 1,)), dma((nz,)),
        ],
        compiler_params=pltpu.CompilerParams(collective_id=0, has_side_effects=True, vmem_limit_bytes=63 * 1024 * 1024),
        name="blocks",
    )(latents, norm_gain, qkv_weight[0], proj_weight[0], merge_weight[0])


def solution(mesh):
    placed = (
        P(None, "seq", None),
        P("section", None),
        P("section", "seq", None),
        P("section", "seq", None),
        P("section", "seq", None),
    )
    return jax.shard_map(
        body, mesh=mesh, in_specs=placed, out_specs=P(None, "seq", "section"), check_vma=False
    )
```

```python
import functools
import math

import jax
import jax.numpy as jnp
from jax import lax
from jax.experimental import pallas as pl
from jax.experimental.pallas import tpu as pltpu
from jax.sharding import PartitionSpec as P

HEAD_DIM = 64
SLICE = 128
CORES = 2
EPSILON = 1e-05
F32 = jnp.float32
BF16 = jnp.bfloat16
MESH = pl.DeviceIdType.MESH


def rcopy(src, dst, send, recv, section, seq):
    return pltpu.make_async_remote_copy(
        src_ref=src,
        dst_ref=dst,
        send_sem=send,
        recv_sem=recv,
        device_id={"section": section, "seq": seq},
        device_id_type=MESH,
    )


def start(copies):
    for copy in copies:
        copy.start()


def wait_send(copies):
    for copy in copies:
        copy.wait_send()


def wait_recv(copies):
    for copy in copies:
        copy.wait_recv()


def kernel(ns, ny, nz, tok, lat_hbm, gain_hbm, qkv_hbm, p_hbm, merge_hbm, out_ref,
           lat_ref, gain_ref, qkv_ref, p_ref, merge_ref, in_sems, w_ref, m_ref, H, A, KV, R, W, MD, WP, skips, O,
           p1s, p1r, m1s, m1r, q1s, q1r, z0r, wzs, wzr, wys, wyr, wcs, wcr,
           mzs, mzr, mys, myr, mcs, mcr, hs, hr, as_, ar, kvs, kvr, kvx, rls, os_, or_):
    nc = CORES
    mid = ns // 2
    dim = ns * SLICE
    zh = nz // 2
    half = zh * tok
    sec = lax.axis_index("section")
    seq = lax.axis_index("seq")
    y = seq // (nz * nc)
    z = (seq // nc) % nz
    c = seq % nc

    def seq_of(y_, z_, c_):
        return y_ * (nz * nc) + z_ * nc + c_

    nx = ns // 2
    farthest = [(dx, dz) for dx in range(nx) for dz in range(2) if (dx, dz) != (0, 0)]
    farthest.sort(key=lambda o: -(min(o[0], nx - o[0]) + o[1]))

    sec_peers = [None] + [lax.rem(sec // nx + dz, 2) * nx + lax.rem(sec + dx, nx) for dx, dz in farthest]
    z_peers = [lax.rem(z + d, nz) for d in range(nz)]
    y_peers = [lax.rem(y + d, ny) for d in range(ny)]

    def sec_peer(d):
        return sec_peers[d]

    def z_peer(d):
        return z_peers[d]

    def y_peer(d):
        return y_peers[d]

    y_order = sorted(range(1, ny), key=lambda d: -min(d, ny - d))
    sibling = seq_of(y, z, 1 - c)

    columns = pl.ds(pl.multiple_of(sec * SLICE, SLICE), SLICE)
    loads = [
        pltpu.make_async_copy(src, dst, in_sems.at[i])
        for i, (src, dst) in enumerate([
            (qkv_hbm, qkv_ref), (gain_hbm, gain_ref), (p_hbm, p_ref), (merge_hbm, merge_ref), (lat_hbm.at[:, :, columns], lat_ref)])
    ]
    start(loads)
    barrier = pltpu.get_barrier_semaphore()
    greeted = [(sec_peer(d), seq) for d in range(1, ns)]
    greeted += [(sec, seq_of(y, z_peer(d), c)) for d in range(1, nz)]
    greeted += [(sec, seq_of(y_peer(d), z, c)) for d in range(1, ny)]
    greeted += [(sec, sibling)]
    for section_, seq_ in greeted:
        pl.semaphore_signal(barrier, inc=1, device_id={"section": section_, "seq": seq_}, device_id_type=MESH)

    for load in loads:
        load.wait()
    part = qkv_ref.shape[0]
    places = lax.broadcasted_iota(jnp.int32, (part, dim), 1) - lax.broadcasted_iota(jnp.int32, (part, dim), 0)
    gain = jnp.sum(jnp.where(places == seq * part, gain_ref[...], 0.0), axis=-1, keepdims=True)
    for j in range(ns):
        for k in range(3):
            at = k * dim + j * SLICE
            piece = qkv_ref[:, at:at + SLICE].astype(F32) * gain
            if k == 0:
                piece = piece * (HEAD_DIM ** (-0.5) * math.log2(math.e))
            w_ref[j, :, k * SLICE:(k + 1) * SLICE] = piece.astype(BF16)
        w_ref[j, :, 3 * SLICE:] = p_ref[:, j * SLICE:(j + 1) * SLICE]
        m_ref[j] = merge_ref[:, j * SLICE:(j + 1) * SLICE]
    pl.semaphore_wait(barrier, len(greeted))

    def first_copies():
        return [rcopy(w_ref.at[sec_peer(d)], W.at[sec, y, z, c], p1s.at[d - 1], p1r.at[sec], sec_peer(d), seq) for d in range(1, ns)]

    def merge_copies():
        return [
            rcopy(m_ref.at[sec_peer(d)], MD.at[sec % mid, y, z, c, sec // mid], m1s.at[d - 1], m1r.at[sec], sec_peer(d), seq)
            for d in range(1, ns)
        ]

    def first_wait(s):
        @pl.when(sec != s)
        def _():
            rcopy(w_ref.at[s], W.at[s, y, z, c], p1s.at[0], p1r.at[s], sec, seq).wait_recv()

    def merge_wait(s):
        @pl.when(sec != s)
        def _():
            rcopy(m_ref.at[s], MD.at[s % mid, y, z, c, s // mid], m1s.at[0], m1r.at[s], sec, seq).wait_recv()

    composed = (sec >= mid - 1) & (sec < ns - 1)

    def proj_copies():
        return [rcopy(p_ref, WP.at[sec - (mid - 1)], q1s.at[d - 1], q1r.at[sec - (mid - 1)], sec_peer(d), seq) for d in range(1, ns)]

    def proj_wait(i):
        @pl.when(sec != i + mid - 1)
        def _():
            rcopy(p_ref, WP.at[i], q1s.at[0], q1r.at[i], sec, seq).wait_recv()

    w_sems = (wzs, wzr, wys, wyr, wcs, wcr)
    m_sems = (mzs, mzr, mys, myr, mcs, mcr)

    def z_copies(ref, sems, s):
        return [rcopy(ref.at[s, y, z, c], ref.at[s, y, z, c], sems[0].at[0], sems[1].at[s], sec, seq_of(y, z_peer(d), c)) for d in range(1, nz)]

    def z_all(ref, sems, s):
        part = ref.at[s, y, pl.ds(0, nz - 1), c]
        return rcopy(part, part, sems[0].at[0], sems[1].at[s], sec, sibling)

    def y_copies(ref, sems, s):
        return [rcopy(ref.at[s, y, :, c], ref.at[s, y, :, c], sems[2].at[0], sems[3].at[s], sec, seq_of(y_peer(d), z, c)) for d in y_order]

    def y_all(ref, sems, s):
        part = ref.at[s, pl.ds(0, ny - 1), :, c]
        return rcopy(part, part, sems[2].at[0], sems[3].at[s], sec, sibling)

    def c_copy(ref, sems, s):
        return rcopy(ref.at[s, :, :, c], ref.at[s, :, :, c], sems[4].at[0], sems[5].at[s], sec, sibling)

    def c_wait(ref, sems, s):
        c_copy(ref, sems, s).wait_send()
        rcopy(ref.at[s, :, :, 1 - c], ref.at[s, :, :, 1 - c], sems[4].at[0], sems[5].at[s], sec, seq).wait_recv()

    def stage_z(ref, sems, s):
        start(z_copies(ref, sems, s))

    def stage_y(ref, sems, s):
        z_all(ref, sems, s).wait_recv()
        start(y_copies(ref, sems, s))
        z_all(ref, sems, s).wait_send()

    def stage_c(ref, sems, s):
        y_all(ref, sems, s).wait_recv()
        c_copy(ref, sems, s).start()
        y_all(ref, sems, s).wait_send()

    def prefetch(stage, s):
        @pl.when(s < ns - 1)
        def _():
            stage(W, w_sems, s + 1)

        @pl.when(s < mid)
        def _():
            stage(MD, m_sems, s)

    def prefetch_z(s):
        @pl.when(s < ns - 1)
        def _():
            @pl.when((s + 1 < mid - 1) | (s + 1 == ns - 1))
            def _():
                first_wait(s + 1)

            stage_z(W, w_sems, s + 1)

        @pl.when(s < mid)
        def _():
            @pl.when(s < mid - 1)
            def _():
                merge_wait(s)

            merge_wait(s + mid)

            @pl.when(s == 0)
            def _():
                merge_wait(mid - 1)
                MD[0, y, z, c, 1] = (MD[0, y, z, c, 1].astype(F32) + MD[mid - 1, y, z, c, 0].astype(F32)).astype(BF16)

            stage_z(MD, m_sems, s)

    def gather_start(buf, ssem, rsem, g):
        start([rcopy(buf.at[g, sec], buf.at[g, sec], ssem.at[g], rsem.at[g], sec_peer(d), seq) for d in range(1, ns)])

    def gather_all(buf, ssem, rsem, g):
        part = buf.at[g, pl.ds(0, ns - 1)]
        return rcopy(part, part, ssem.at[g], rsem.at[g], sec, sibling)

    def kv_start(par, g):
        own = KV.at[par, g, c, y]
        start([rcopy(own, own, kvs.at[g], kvr.at[par, g, y], sec, seq_of(y_peer(d), z, c)) for d in y_order])
        rcopy(own, own, kvs.at[g], kvx.at[par, g], sec, sibling).start()

    def kv_sent(par, g):
        part = KV.at[par, g, c, pl.ds(0, ny)]
        rcopy(part, part, kvs.at[g], kvx.at[par, g], sec, sibling).wait_send()
        part = KV.at[par, g, c, pl.ds(0, ny - 1)]
        rcopy(part, part, rls.at[g], kvx.at[par, g], sec, sibling).wait_send()

    def kv_relay(par, g, d):
        p = y_peer(d)
        slot = KV.at[par, g, c, p]
        rcopy(slot, slot, rls.at[g], kvr.at[par, g, p], sec, sibling).wait_recv()
        rcopy(slot, slot, rls.at[g], kvx.at[par, g], sec, sibling).start()

    def kv_other(par, g):
        part = KV.at[par, g, 1 - c, pl.ds(0, ny)]
        rcopy(part, part, kvs.at[g], kvx.at[par, g], sec, sibling).wait_recv()

    def rows_of(z_):
        return pl.ds(lax.rem(z_, zh) * tok, tok)

    def local_rows(z_):
        return pl.ds(pl.multiple_of(lax.rem(z_, zh) * tok, tok), tok)

    @pl.when(sec == 0)
    def _():
        start(first_copies())

    lat_copies = [
        rcopy(lat_ref.at[z_peer(d)], H.at[z // zh, sec, rows_of(z)], os_.at[d - 1], or_.at[z], sec, seq_of(y, z_peer(d), c))
        for d in range(1, nz)
    ]
    start(lat_copies)
    W[sec, y, z, c] = w_ref[sec]
    MD[sec % mid, y, z, c, sec // mid] = m_ref[sec]
    H[z // zh, sec, local_rows(z), :] = lat_ref[z]

    @pl.when(composed)
    def _():
        WP[sec - (mid - 1)] = p_ref[...]

    first_wait(0)

    def along_y(z_):
        return [rcopy(W.at[0, y, z_, c], W.at[0, y, z_, c], wys.at[0], wyr.at[0], sec, seq_of(y_peer(d), z, c)) for d in y_order]

    start([rcopy(W.at[0, y, z, c], W.at[0, y, z, c], wzs.at[0], z0r.at[z], sec, seq_of(y, z_peer(d), c)) for d in range(1, nz)])
    start(along_y(z))
    for d in range(1, nz):
        p = z_peer(d)
        rcopy(lat_ref.at[p], H.at[p // zh, sec, rows_of(p)], os_.at[d - 1], or_.at[p], sec, seq).wait_recv()
    gather_start(H, hs, hr, 0)
    for d in sorted(range(1, nz), key=lambda d: min(d, nz - d)):
        p = z_peer(d)
        rcopy(W.at[0, y, p, c], W.at[0, y, p, c], wzs.at[0], z0r.at[p], sec, seq).wait_recv()
        start(along_y(p))
    gather_start(H, hs, hr, 1)

    @pl.when(sec != 0)
    def _():
        start(first_copies())

    start(merge_copies())
    z_all(W, w_sems, 0).wait_send()
    wait_send(lat_copies)
    skips[mid - 1] = jnp.zeros((2, half, SLICE), BF16)
    stage_c(W, w_sems, 0)

    def weights(s, lo, hi):
        return W[s, :, :, :, :, lo:hi].reshape(dim, hi - lo)

    def merge_weights(s, which):
        return MD[s, :, :, :, which].reshape(dim, SLICE)

    def whole(buf, g):
        return jnp.concatenate([buf[g, p] for p in range(ns)], axis=1)

    lane = lax.broadcasted_iota(jnp.int32, (half, SLICE), 1)
    def block(s, carry):
        par = lax.rem(s, 2)
        c_wait(W, w_sems, s)

        stacked = []
        for g in range(2):
            gather_all(H, hs, hr, g).wait_recv()
            total = jnp.zeros((half, SLICE), F32)
            for p in range(ns):
                total = total + H[g, p].astype(F32)
            mean = jnp.sum(total, axis=-1, keepdims=True) * (1.0 / dim)
            total = jnp.zeros((half, SLICE), F32)
            for p in range(ns):
                center = H[g, p].astype(F32) - mean
                total = total + center * center
            spread = jnp.sum(total, axis=-1, keepdims=True) * (1.0 / dim)
            inverse = lax.rsqrt(spread + EPSILON)
            normed = jnp.concatenate([((H[g, p].astype(F32) - mean) * inverse).astype(BF16) for p in range(ns)], axis=1)
            kv = jnp.dot(normed, weights(s, 128, 384), preferred_element_type=F32)
            KV[par, g, c, y] = kv.astype(BF16)
            kv_start(par, g)
            q = jnp.dot(normed, weights(s, 0, 128), preferred_element_type=F32)
            stacked.append(jnp.concatenate([jnp.where(lane < HEAD_DIM, q, 0.0), jnp.where(lane < HEAD_DIM, 0.0, q)], axis=0).astype(BF16))

        prefetch_z(s)

        @pl.when((s >= 1) & (s <= mid))
        def _():
            c_wait(MD, m_sems, s - 1)

        @pl.when((s == 0) & composed)
        def _():
            start(proj_copies())

        for g in range(2):
            @pl.when((s >= mid - 1) & (s < ns - 1))
            def _():
                merged = jnp.dot(whole(H, g), merge_weights(s - (mid - 1), 1), preferred_element_type=F32)
                R[g] = merged + skips[ns - 2 - s, g].astype(F32)

            @pl.when((s < mid - 1) | (s == ns - 1))
            def _():
                R[g] = H[g, sec].astype(F32)

            @pl.when((s >= 1) & (s < mid))
            def _():
                skips[s - 1, g] = jnp.dot(whole(H, g), merge_weights(s - 1, 0), preferred_element_type=F32).astype(BF16)

        @pl.when(s == 1)
        def _():
            for i in range(mid):
                proj_wait(i)

            @pl.when(composed)
            def _():
                wait_send(proj_copies())

        @pl.when((s >= 1) & (s <= mid))
        def _():
            first_wait(s + mid - 2)
            rows = jnp.dot(WP[s - 1], merge_weights(s - 1, 1), preferred_element_type=F32)
            W[s + mid - 2, y, z, c, :, 384:512] = rows.astype(BF16)

        tops, sums, mixes = [None, None], [None, None], [None, None]

        def attend(gq, g, cores):
            keys = jnp.concatenate([KV[par, g, core, :, :, 0:SLICE].reshape(ny * half, SLICE) for core in cores], axis=0)
            vals = jnp.concatenate([KV[par, g, core, :, :, SLICE:2 * SLICE].reshape(ny * half, SLICE) for core in cores], axis=0)
            scores = lax.dot_general(stacked[gq], keys, (((1,), (1,)), ((), ())), preferred_element_type=F32)
            top = jnp.max(scores, axis=-1, keepdims=True)
            if tops[gq] is not None:
                top = jnp.maximum(tops[gq], top)
            e = jnp.exp2(scores - top)
            mix = jnp.dot(e.astype(BF16), vals, preferred_element_type=F32)
            total = jnp.sum(e, axis=-1, keepdims=True)
            if tops[gq] is not None:
                fade = jnp.exp2(tops[gq] - top)
                mix = mixes[gq] * fade + mix
                total = sums[gq] * fade + total
            tops[gq], sums[gq], mixes[gq] = top, total, mix

        for g in range(2):
            for d in reversed(y_order):
                kv_relay(par, g, d)
            if g == 1:
                prefetch(stage_y, s)
                for half_ in range(2):
                    gather_all(H, hs, hr, half_).wait_send()
            kv_other(par, g)
            for gq in range(2):
                attend(gq, g, [0, 1])
                if g == 1:
                    mix = mixes[gq] / sums[gq]
                    A[gq, sec] = jnp.where(lane < HEAD_DIM, mix[:half], mix[half:]).astype(BF16)
                    gather_start(A, as_, ar, gq)
        for g in range(2):
            kv_sent(par, g)

        for g in range(2):
            gather_all(A, as_, ar, g).wait_recv()
            update = jnp.dot(whole(A, g), weights(s, 384, 512), preferred_element_type=F32)
            H[g, sec] = (R[g] + update).astype(BF16)

            @pl.when(s < ns - 1)
            def _():
                gather_start(H, hs, hr, g)

        prefetch(stage_c, s)
        for g in range(2):
            gather_all(A, as_, ar, g).wait_send()
        return carry

    lax.fori_loop(0, ns, block, 0)

    out_copies = [
        rcopy(H.at[z_peer(d) // zh, sec, rows_of(z_peer(d))], O.at[z], os_.at[d - 1], or_.at[z], sec, seq_of(y, z_peer(d), c))
        for d in range(1, nz)
    ]
    start(out_copies)
    O[z] = H[z // zh, sec, local_rows(z), :]
    wait_recv([rcopy(O.at[z_peer(d)], O.at[z_peer(d)], os_.at[d - 1], or_.at[z_peer(d)], sec, seq) for d in range(1, nz)])
    out_ref[...] = O[...]
    wait_send(first_copies())
    wait_send(merge_copies())
    wait_send(out_copies)


def body(latents, norm_gain, qkv_weight, proj_weight, merge_weight):
    windows, tok, dim = latents.shape
    ns = lax.axis_size("section")
    nseq = lax.axis_size("seq")
    nz = windows
    ny = nseq // (nz * CORES)
    part = dim // nseq
    half = nz * tok // 2
    mid = ns // 2
    dma = pltpu.SemaphoreType.DMA
    vmem = pl.BlockSpec(memory_space=pltpu.VMEM)
    gather_sems = [dma((2,)), dma((2,))]
    w_sems = [dma((1,)), dma((ns,)), dma((1,)), dma((ns,)), dma((1,)), dma((ns,))]
    return pl.pallas_call(
        functools.partial(kernel, ns, ny, nz, tok),
        out_shape=jax.ShapeDtypeStruct((nz, tok, SLICE), BF16),
        in_specs=[pl.BlockSpec(memory_space=pltpu.MemorySpace.HBM)] * 5,
        out_specs=vmem,
        scratch_shapes=[
            pltpu.VMEM((nz, tok, SLICE), BF16),
            pltpu.VMEM((1, dim), F32),
            pltpu.VMEM((part, 3 * dim), BF16),
            pltpu.VMEM((part, dim), BF16),
            pltpu.VMEM((part, dim), BF16),
            dma((5,)),
            pltpu.VMEM((ns, part, 4 * SLICE), BF16),
            pltpu.VMEM((ns, part, SLICE), BF16),
            pltpu.VMEM((2, ns, half, SLICE), BF16),
            pltpu.VMEM((2, ns, half, SLICE), BF16),
            pltpu.VMEM((2, 2, CORES, ny, half, 2 * SLICE), BF16),
            pltpu.VMEM((2, half, SLICE), F32),
            pltpu.VMEM((ns, ny, nz, CORES, part, 4 * SLICE), BF16),
            pltpu.VMEM((mid, ny, nz, CORES, 2, part, SLICE), BF16),
            pltpu.VMEM((mid, part, dim), BF16),
            pltpu.VMEM((mid, 2, half, SLICE), BF16),
            pltpu.VMEM((nz, tok, SLICE), BF16),
            dma((ns - 1,)), dma((ns,)),
            dma((ns - 1,)), dma((ns,)),
            dma((ns - 1,)), dma((mid,)),
            dma((nz,)),
            *w_sems,
            *w_sems,
            *gather_sems,
            *gather_sems,
            dma((2,)), dma((2, 2, ny)), dma((2, 2)), dma((2,)),
            dma((nz - 1,)), dma((nz,)),
        ],
        compiler_params=pltpu.CompilerParams(collective_id=0, has_side_effects=True, vmem_limit_bytes=63 * 1024 * 1024),
        name="blocks",
    )(latents, norm_gain, qkv_weight[0], proj_weight[0], merge_weight[0])


def solution(mesh):
    placed = (
        P(None, "seq", None),
        P("section", None),
        P("section", "seq", None),
        P("section", "seq", None),
        P("section", "seq", None),
    )
    return jax.shard_map(
        body, mesh=mesh, in_specs=placed, out_specs=P(None, "seq", "section"), check_vma=False
    )
```

```python
import functools
import math

import jax
import jax.numpy as jnp
from jax import lax
from jax.experimental import pallas as pl
from jax.experimental.pallas import tpu as pltpu
from jax.sharding import PartitionSpec as P

HEAD_DIM = 64
SLICE = 128
CORES = 2
EPSILON = 1e-05
F32 = jnp.float32
BF16 = jnp.bfloat16
MESH = pl.DeviceIdType.MESH


def rcopy(src, dst, send, recv, section, seq):
    return pltpu.make_async_remote_copy(
        src_ref=src,
        dst_ref=dst,
        send_sem=send,
        recv_sem=recv,
        device_id={"section": section, "seq": seq},
        device_id_type=MESH,
    )


def start(copies):
    for copy in copies:
        copy.start()


def wait_send(copies):
    for copy in copies:
        copy.wait_send()


def wait_recv(copies):
    for copy in copies:
        copy.wait_recv()


def kernel(ns, ny, nz, tok, lat_hbm, gain_hbm, qkv_hbm, p_hbm, merge_hbm, out_ref,
           lat_ref, gain_ref, qkv_ref, p_ref, merge_ref, in_sems, w_ref, m_ref, H, A, KV, R, W, MD, WP, skips, O,
           p1s, p1r, m1s, m1r, q1s, q1r, z0r, wzs, wzr, wys, wyr, wcs, wcr,
           mzs, mzr, mys, myr, mcs, mcr, hs, hr, as_, ar, kvs, kvr, kvx, rls, os_, or_):
    nc = CORES
    mid = ns // 2
    dim = ns * SLICE
    zh = nz // 2
    half = zh * tok
    sec = lax.axis_index("section")
    seq = lax.axis_index("seq")
    y = seq // (nz * nc)
    z = (seq // nc) % nz
    c = seq % nc

    def seq_of(y_, z_, c_):
        return y_ * (nz * nc) + z_ * nc + c_

    nx = ns // 2
    farthest = [(dx, dz) for dx in range(nx) for dz in range(2) if (dx, dz) != (0, 0)]
    farthest.sort(key=lambda o: -(min(o[0], nx - o[0]) + o[1]))

    sec_peers = [None] + [lax.rem(sec // nx + dz, 2) * nx + lax.rem(sec + dx, nx) for dx, dz in farthest]
    z_peers = [lax.rem(z + d, nz) for d in range(nz)]
    y_peers = [lax.rem(y + d, ny) for d in range(ny)]

    def sec_peer(d):
        return sec_peers[d]

    def z_peer(d):
        return z_peers[d]

    def y_peer(d):
        return y_peers[d]

    y_order = sorted(range(1, ny), key=lambda d: -min(d, ny - d))
    sibling = seq_of(y, z, 1 - c)

    columns = pl.ds(pl.multiple_of(sec * SLICE, SLICE), SLICE)
    loads = [
        pltpu.make_async_copy(src, dst, in_sems.at[i])
        for i, (src, dst) in enumerate([
            (qkv_hbm, qkv_ref), (gain_hbm, gain_ref), (p_hbm, p_ref), (merge_hbm, merge_ref), (lat_hbm.at[:, :, columns], lat_ref)])
    ]
    start(loads)
    barrier = pltpu.get_barrier_semaphore()
    greeted = [(sec_peer(d), seq) for d in range(1, ns)]
    greeted += [(sec, seq_of(y, z_peer(d), c)) for d in range(1, nz)]
    greeted += [(sec, seq_of(y_peer(d), z, c)) for d in range(1, ny)]
    greeted += [(sec, sibling)]
    for section_, seq_ in greeted:
        pl.semaphore_signal(barrier, inc=1, device_id={"section": section_, "seq": seq_}, device_id_type=MESH)

    for load in loads:
        load.wait()
    part = qkv_ref.shape[0]
    places = lax.broadcasted_iota(jnp.int32, (part, dim), 1) - lax.broadcasted_iota(jnp.int32, (part, dim), 0)
    gain = jnp.sum(jnp.where(places == seq * part, gain_ref[...], 0.0), axis=-1, keepdims=True)
    for j in range(ns):
        for k in range(3):
            at = k * dim + j * SLICE
            piece = qkv_ref[:, at:at + SLICE].astype(F32) * gain
            if k == 0:
                piece = piece * (HEAD_DIM ** (-0.5) * math.log2(math.e))
            w_ref[j, :, k * SLICE:(k + 1) * SLICE] = piece.astype(BF16)
        w_ref[j, :, 3 * SLICE:] = p_ref[:, j * SLICE:(j + 1) * SLICE]
        m_ref[j] = merge_ref[:, j * SLICE:(j + 1) * SLICE]
    pl.semaphore_wait(barrier, len(greeted))

    def first_copies():
        return [rcopy(w_ref.at[sec_peer(d)], W.at[sec, y, z, c], p1s.at[d - 1], p1r.at[sec], sec_peer(d), seq) for d in range(1, ns)]

    def merge_copies():
        return [
            rcopy(m_ref.at[sec_peer(d)], MD.at[sec % mid, y, z, c, sec // mid], m1s.at[d - 1], m1r.at[sec], sec_peer(d), seq)
            for d in range(1, ns)
        ]

    def first_wait(s):
        @pl.when(sec != s)
        def _():
            rcopy(w_ref.at[s], W.at[s, y, z, c], p1s.at[0], p1r.at[s], sec, seq).wait_recv()

    def merge_wait(s):
        @pl.when(sec != s)
        def _():
            rcopy(m_ref.at[s], MD.at[s % mid, y, z, c, s // mid], m1s.at[0], m1r.at[s], sec, seq).wait_recv()

    composed = (sec >= mid - 1) & (sec < ns - 1)

    def proj_copies():
        return [rcopy(p_ref, WP.at[sec - (mid - 1)], q1s.at[d - 1], q1r.at[sec - (mid - 1)], sec_peer(d), seq) for d in range(1, ns)]

    def proj_wait(i):
        @pl.when(sec != i + mid - 1)
        def _():
            rcopy(p_ref, WP.at[i], q1s.at[0], q1r.at[i], sec, seq).wait_recv()

    w_sems = (wzs, wzr, wys, wyr, wcs, wcr)
    m_sems = (mzs, mzr, mys, myr, mcs, mcr)

    def z_copies(ref, sems, s):
        return [rcopy(ref.at[s, y, z, c], ref.at[s, y, z, c], sems[0].at[0], sems[1].at[s], sec, seq_of(y, z_peer(d), c)) for d in range(1, nz)]

    def z_all(ref, sems, s):
        part = ref.at[s, y, pl.ds(0, nz - 1), c]
        return rcopy(part, part, sems[0].at[0], sems[1].at[s], sec, sibling)

    def y_copies(ref, sems, s):
        return [rcopy(ref.at[s, y, :, c], ref.at[s, y, :, c], sems[2].at[0], sems[3].at[s], sec, seq_of(y_peer(d), z, c)) for d in y_order]

    def y_all(ref, sems, s):
        part = ref.at[s, pl.ds(0, ny - 1), :, c]
        return rcopy(part, part, sems[2].at[0], sems[3].at[s], sec, sibling)

    def c_copy(ref, sems, s):
        return rcopy(ref.at[s, :, :, c], ref.at[s, :, :, c], sems[4].at[0], sems[5].at[s], sec, sibling)

    def c_wait(ref, sems, s):
        c_copy(ref, sems, s).wait_send()
        rcopy(ref.at[s, :, :, 1 - c], ref.at[s, :, :, 1 - c], sems[4].at[0], sems[5].at[s], sec, seq).wait_recv()

    def stage_z(ref, sems, s):
        start(z_copies(ref, sems, s))

    def stage_y(ref, sems, s):
        z_all(ref, sems, s).wait_recv()
        start(y_copies(ref, sems, s))
        z_all(ref, sems, s).wait_send()

    def stage_c(ref, sems, s):
        y_all(ref, sems, s).wait_recv()
        c_copy(ref, sems, s).start()
        y_all(ref, sems, s).wait_send()

    def prefetch(stage, s):
        @pl.when(s < ns - 1)
        def _():
            stage(W, w_sems, s + 1)

        @pl.when(s < mid)
        def _():
            stage(MD, m_sems, s)

    def prefetch_z(s):
        @pl.when(s < ns - 1)
        def _():
            @pl.when((s + 1 < mid - 1) | (s + 1 == ns - 1))
            def _():
                first_wait(s + 1)

            stage_z(W, w_sems, s + 1)

        @pl.when(s < mid)
        def _():
            @pl.when(s < mid - 1)
            def _():
                merge_wait(s)

            merge_wait(s + mid)

            @pl.when(s == 0)
            def _():
                merge_wait(mid - 1)
                MD[0, y, z, c, 1] = (MD[0, y, z, c, 1].astype(F32) + MD[mid - 1, y, z, c, 0].astype(F32)).astype(BF16)

            stage_z(MD, m_sems, s)

    def gather_start(buf, ssem, rsem, g):
        start([rcopy(buf.at[g, sec], buf.at[g, sec], ssem.at[g], rsem.at[g], sec_peer(d), seq) for d in range(1, ns)])

    def gather_all(buf, ssem, rsem, g):
        part = buf.at[g, pl.ds(0, ns - 1)]
        return rcopy(part, part, ssem.at[g], rsem.at[g], sec, sibling)

    def kv_start(par, g):
        own = KV.at[par, g, c, y]
        start([rcopy(own, own, kvs.at[g], kvr.at[par, g, y], sec, seq_of(y_peer(d), z, c)) for d in y_order])
        rcopy(own, own, kvs.at[g], kvx.at[par, g], sec, sibling).start()

    def kv_sent(par, g):
        part = KV.at[par, g, c, pl.ds(0, ny)]
        rcopy(part, part, kvs.at[g], kvx.at[par, g], sec, sibling).wait_send()
        part = KV.at[par, g, c, pl.ds(0, ny - 1)]
        rcopy(part, part, rls.at[g], kvx.at[par, g], sec, sibling).wait_send()

    def kv_relay(par, g, d):
        p = y_peer(d)
        slot = KV.at[par, g, c, p]
        rcopy(slot, slot, rls.at[g], kvr.at[par, g, p], sec, sibling).wait_recv()
        rcopy(slot, slot, rls.at[g], kvx.at[par, g], sec, sibling).start()

    def kv_other(par, g):
        part = KV.at[par, g, 1 - c, pl.ds(0, ny)]
        rcopy(part, part, kvs.at[g], kvx.at[par, g], sec, sibling).wait_recv()

    def rows_of(z_):
        return pl.ds(lax.rem(z_, zh) * tok, tok)

    def local_rows(z_):
        return pl.ds(pl.multiple_of(lax.rem(z_, zh) * tok, tok), tok)

    @pl.when(sec == 0)
    def _():
        start(first_copies())

    lat_copies = [
        rcopy(lat_ref.at[z_peer(d)], H.at[z // zh, sec, rows_of(z)], os_.at[d - 1], or_.at[z], sec, seq_of(y, z_peer(d), c))
        for d in range(1, nz)
    ]
    start(lat_copies)
    W[sec, y, z, c] = w_ref[sec]
    MD[sec % mid, y, z, c, sec // mid] = m_ref[sec]
    H[z // zh, sec, local_rows(z), :] = lat_ref[z]

    @pl.when(composed)
    def _():
        WP[sec - (mid - 1)] = p_ref[...]

    first_wait(0)

    def along_y(z_):
        return [rcopy(W.at[0, y, z_, c], W.at[0, y, z_, c], wys.at[0], wyr.at[0], sec, seq_of(y_peer(d), z, c)) for d in y_order]

    start([rcopy(W.at[0, y, z, c], W.at[0, y, z, c], wzs.at[0], z0r.at[z], sec, seq_of(y, z_peer(d), c)) for d in range(1, nz)])
    start(along_y(z))
    for d in range(1, nz):
        p = z_peer(d)
        rcopy(lat_ref.at[p], H.at[p // zh, sec, rows_of(p)], os_.at[d - 1], or_.at[p], sec, seq).wait_recv()
    gather_start(H, hs, hr, 0)
    for d in sorted(range(1, nz), key=lambda d: min(d, nz - d)):
        p = z_peer(d)
        rcopy(W.at[0, y, p, c], W.at[0, y, p, c], wzs.at[0], z0r.at[p], sec, seq).wait_recv()
        start(along_y(p))
    gather_start(H, hs, hr, 1)

    @pl.when(sec != 0)
    def _():
        start(first_copies())

    start(merge_copies())
    z_all(W, w_sems, 0).wait_send()
    wait_send(lat_copies)
    skips[mid - 1] = jnp.zeros((2, half, SLICE), BF16)
    stage_c(W, w_sems, 0)

    def weights(s, lo, hi):
        return W[s, :, :, :, :, lo:hi].reshape(dim, hi - lo)

    def merge_weights(s, which):
        return MD[s, :, :, :, which].reshape(dim, SLICE)

    def whole(buf, g):
        return jnp.concatenate([buf[g, p] for p in range(ns)], axis=1)

    lane = lax.broadcasted_iota(jnp.int32, (half, SLICE), 1)
    def block(s, carry):
        par = lax.rem(s, 2)

        stacked = []
        for g in range(2):
            gather_all(H, hs, hr, g).wait_recv()
            total = jnp.zeros((half, SLICE), F32)
            for p in range(ns):
                total = total + H[g, p].astype(F32)
            mean = jnp.sum(total, axis=-1, keepdims=True) * (1.0 / dim)
            total = jnp.zeros((half, SLICE), F32)
            for p in range(ns):
                center = H[g, p].astype(F32) - mean
                total = total + center * center
            spread = jnp.sum(total, axis=-1, keepdims=True) * (1.0 / dim)
            inverse = lax.rsqrt(spread + EPSILON)
            normed = jnp.concatenate([((H[g, p].astype(F32) - mean) * inverse).astype(BF16) for p in range(ns)], axis=1)
            if g == 0:
                c_wait(W, w_sems, s)
            kv = jnp.dot(normed, weights(s, 128, 384), preferred_element_type=F32)
            KV[par, g, c, y] = kv.astype(BF16)
            kv_start(par, g)
            q = jnp.dot(normed, weights(s, 0, 128), preferred_element_type=F32)
            stacked.append(jnp.concatenate([jnp.where(lane < HEAD_DIM, q, 0.0), jnp.where(lane < HEAD_DIM, 0.0, q)], axis=0).astype(BF16))

        prefetch_z(s)

        @pl.when((s >= 1) & (s <= mid))
        def _():
            c_wait(MD, m_sems, s - 1)

        @pl.when((s == 0) & composed)
        def _():
            start(proj_copies())

        for g in range(2):
            @pl.when((s >= mid - 1) & (s < ns - 1))
            def _():
                merged = jnp.dot(whole(H, g), merge_weights(s - (mid - 1), 1), preferred_element_type=F32)
                R[g] = merged + skips[ns - 2 - s, g].astype(F32)

            @pl.when((s < mid - 1) | (s == ns - 1))
            def _():
                R[g] = H[g, sec].astype(F32)

            @pl.when((s >= 1) & (s < mid))
            def _():
                skips[s - 1, g] = jnp.dot(whole(H, g), merge_weights(s - 1, 0), preferred_element_type=F32).astype(BF16)

        @pl.when(s == 1)
        def _():
            for i in range(mid):
                proj_wait(i)

            @pl.when(composed)
            def _():
                wait_send(proj_copies())

        @pl.when((s >= 1) & (s <= mid))
        def _():
            first_wait(s + mid - 2)
            rows = jnp.dot(WP[s - 1], merge_weights(s - 1, 1), preferred_element_type=F32)
            W[s + mid - 2, y, z, c, :, 384:512] = rows.astype(BF16)

        tops, sums, mixes = [None, None], [None, None], [None, None]

        def attend(gq, g, cores):
            keys = jnp.concatenate([KV[par, g, core, :, :, 0:SLICE].reshape(ny * half, SLICE) for core in cores], axis=0)
            vals = jnp.concatenate([KV[par, g, core, :, :, SLICE:2 * SLICE].reshape(ny * half, SLICE) for core in cores], axis=0)
            scores = lax.dot_general(stacked[gq], keys, (((1,), (1,)), ((), ())), preferred_element_type=F32)
            top = jnp.max(scores, axis=-1, keepdims=True)
            if tops[gq] is not None:
                top = jnp.maximum(tops[gq], top)
            e = jnp.exp2(scores - top)
            mix = jnp.dot(e.astype(BF16), vals, preferred_element_type=F32)
            total = jnp.sum(e, axis=-1, keepdims=True)
            if tops[gq] is not None:
                fade = jnp.exp2(tops[gq] - top)
                mix = mixes[gq] * fade + mix
                total = sums[gq] * fade + total
            tops[gq], sums[gq], mixes[gq] = top, total, mix

        for g in range(2):
            for d in reversed(y_order):
                kv_relay(par, g, d)
            if g == 1:
                prefetch(stage_y, s)
                for half_ in range(2):
                    gather_all(H, hs, hr, half_).wait_send()
            kv_other(par, g)
            for gq in range(2):
                attend(gq, g, [0, 1])
                if g == 1:
                    mix = mixes[gq] / sums[gq]
                    A[gq, sec] = jnp.where(lane < HEAD_DIM, mix[:half], mix[half:]).astype(BF16)
                    gather_start(A, as_, ar, gq)
        for g in range(2):
            kv_sent(par, g)

        for g in range(2):
            gather_all(A, as_, ar, g).wait_recv()
            update = jnp.dot(whole(A, g), weights(s, 384, 512), preferred_element_type=F32)
            H[g, sec] = (R[g] + update).astype(BF16)

            @pl.when(s < ns - 1)
            def _():
                gather_start(H, hs, hr, g)

        prefetch(stage_c, s)
        for g in range(2):
            gather_all(A, as_, ar, g).wait_send()
        return carry

    lax.fori_loop(0, ns, block, 0)

    out_copies = [
        rcopy(H.at[z_peer(d) // zh, sec, rows_of(z_peer(d))], O.at[z], os_.at[d - 1], or_.at[z], sec, seq_of(y, z_peer(d), c))
        for d in range(1, nz)
    ]
    start(out_copies)
    O[z] = H[z // zh, sec, local_rows(z), :]
    wait_recv([rcopy(O.at[z_peer(d)], O.at[z_peer(d)], os_.at[d - 1], or_.at[z_peer(d)], sec, seq) for d in range(1, nz)])
    out_ref[...] = O[...]
    wait_send(first_copies())
    wait_send(merge_copies())
    wait_send(out_copies)


def body(latents, norm_gain, qkv_weight, proj_weight, merge_weight):
    windows, tok, dim = latents.shape
    ns = lax.axis_size("section")
    nseq = lax.axis_size("seq")
    nz = windows
    ny = nseq // (nz * CORES)
    part = dim // nseq
    half = nz * tok // 2
    mid = ns // 2
    dma = pltpu.SemaphoreType.DMA
    vmem = pl.BlockSpec(memory_space=pltpu.VMEM)
    gather_sems = [dma((2,)), dma((2,))]
    w_sems = [dma((1,)), dma((ns,)), dma((1,)), dma((ns,)), dma((1,)), dma((ns,))]
    return pl.pallas_call(
        functools.partial(kernel, ns, ny, nz, tok),
        out_shape=jax.ShapeDtypeStruct((nz, tok, SLICE), BF16),
        in_specs=[pl.BlockSpec(memory_space=pltpu.MemorySpace.HBM)] * 5,
        out_specs=vmem,
        scratch_shapes=[
            pltpu.VMEM((nz, tok, SLICE), BF16),
            pltpu.VMEM((1, dim), F32),
            pltpu.VMEM((part, 3 * dim), BF16),
            pltpu.VMEM((part, dim), BF16),
            pltpu.VMEM((part, dim), BF16),
            dma((5,)),
            pltpu.VMEM((ns, part, 4 * SLICE), BF16),
            pltpu.VMEM((ns, part, SLICE), BF16),
            pltpu.VMEM((2, ns, half, SLICE), BF16),
            pltpu.VMEM((2, ns, half, SLICE), BF16),
            pltpu.VMEM((2, 2, CORES, ny, half, 2 * SLICE), BF16),
            pltpu.VMEM((2, half, SLICE), F32),
            pltpu.VMEM((ns, ny, nz, CORES, part, 4 * SLICE), BF16),
            pltpu.VMEM((mid, ny, nz, CORES, 2, part, SLICE), BF16),
            pltpu.VMEM((mid, part, dim), BF16),
            pltpu.VMEM((mid, 2, half, SLICE), BF16),
            pltpu.VMEM((nz, tok, SLICE), BF16),
            dma((ns - 1,)), dma((ns,)),
            dma((ns - 1,)), dma((ns,)),
            dma((ns - 1,)), dma((mid,)),
            dma((nz,)),
            *w_sems,
            *w_sems,
            *gather_sems,
            *gather_sems,
            dma((2,)), dma((2, 2, ny)), dma((2, 2)), dma((2,)),
            dma((nz - 1,)), dma((nz,)),
        ],
        compiler_params=pltpu.CompilerParams(collective_id=0, has_side_effects=True, vmem_limit_bytes=63 * 1024 * 1024),
        name="blocks",
    )(latents, norm_gain, qkv_weight[0], proj_weight[0], merge_weight[0])


def solution(mesh):
    placed = (
        P(None, "seq", None),
        P("section", None),
        P("section", "seq", None),
        P("section", "seq", None),
        P("section", "seq", None),
    )
    return jax.shard_map(
        body, mesh=mesh, in_specs=placed, out_specs=P(None, "seq", "section"), check_vma=False
    )
```
